256 devices in a mesh: ctx: 32 (over z, x), tp: 8 (over y, core).
Axes of the slice: x: 4, y: 4, z: 8, core: 2. Of those that a mesh axis runs over, the one named last changes fastest.
Arguments:
- embeds: bfloat16 [3, 8, 8192], P(None, None, 'ctx')
- norm_mamba: float32 [8192], P('ctx'), may hold values from 0.1 to 1.9
- in_x: bfloat16 [8192, 16384], P('ctx', 'tp'), may hold values from -0.0625 to 0.0625
- in_z: bfloat16 [8192, 16384], P('ctx', 'tp'), may hold values from -0.0625 to 0.0625
- conv_w: float32 [4, 16384], P(None, 'tp'), may hold values from -3 to 3
- conv_b: float32 [16384], P('tp'), may hold values from -3 to 3
- x_proj: bfloat16 [16384, 544], P('tp'), may hold values from -0.046875 to 0.046875
- dt_norm: float32 [512], replicated, may hold values from 0.1 to 1.9
- b_norm: float32 [16], replicated, may hold values from 0.1 to 1.9
- c_norm: float32 [16], replicated, may hold values from 0.1 to 1.9
- dt_proj: bfloat16 [512, 16384], P(None, 'tp'), may hold values from -0.25 to 0.25
- dt_bias: float32 [16384], P('tp'), may hold values from -3 to 0
- a_log: float32 [16, 16384], P(None, 'tp'), may hold values from 0 to 2.77
- d_skip: float32 [16384], P('tp'), may hold values from 0.5 to 1.5
- out_proj: bfloat16 [16384, 8192], P('tp', 'ctx'), may hold values from -0.046875 to 0.046875
- norm_attn: float32 [8192], P('ctx'), may hold values from 0.1 to 1.9
- w_query: bfloat16 [8192, 8192], P('ctx', 'tp'), may hold values from -0.0625 to 0.0625
- key_matrix: bfloat16 [8192, 1024], P('ctx', 'tp'), may hold values from -0.0625 to 0.0625
- value_matrix: bfloat16 [8192, 1024], P('ctx', 'tp'), may hold values from -0.0625 to 0.0625
- w_out: bfloat16 [8192, 8192], P('tp', 'ctx'), may hold values from -0.0625 to 0.0625
- cache_k: bfloat16 [8, 16384, 1024], P(None, 'ctx', 'tp')
- value_cache: bfloat16 [8, 16384, 1024], P(None, 'ctx', 'tp'), may hold values from -6 to 6
- lengths: int32 [8], replicated, may hold values from 1 to 16384, as said below
- block_of_slot: int32 [8, 128], P(None, 'ctx'), may hold values from 0 to 127, as said below
- conv_state: float32 [8, 3, 16384], P(None, None, 'tp'), may hold values from -6 to 6
- ssm_state: float32 [8, 16, 16384], P(None, None, 'tp'), may hold values from -6 to 6
Outputs:
- hidden_out: float32 [3, 8, 8192], P(None, None, 'ctx')
- new_keys: bfloat16 [3, 8, 1024], P(None, None, 'tp')
- new_values: bfloat16 [3, 8, 1024], P(None, None, 'tp')
- ssm_out: float32 [8, 16, 16384], P(None, None, 'tp')
- conv_out: float32 [8, 3, 16384], P(None, None, 'tp')
The draws below stay inside these ranges and needn't reach their ends.
Inputs may be any that keep to these rules, and one draw needn't show every extreme that they name: Each row of block_of_slot is a permutation of 0 .. 127. `lengths`: some row has all 16384 slots filled.
All inputs are finite; a program needn't handle non-finite values.
Results may differ from the reference program's by a relative error of at most 0.025.
Values may be sent and summed in bfloat16 or wider, within the bound.
No kernel may reach another device: no remote copies, remote signals or barrier semaphores. Data moves between devices by JAX's collectives and lax.ppermute only.
A program may use at most 128 MiB of HBM per device.

```python
import jax
import jax.numpy as jnp
from jax import lax

MODEL_WIDTH = 8192
DI = 16384
DS = 16
DTR = 512
CONV = 4
QUERY_HEADS = 64
KEY_VALUE_HEADS = 8
HEAD_SIZE = 128
BLK = 128
STEPS = 3
BATCH_ROW_COUNT = 8
CACHE_SLOTS = 16384
NBLK = 128


def draw_embeds(key, part):
    key = jax.random.fold_in(key, 11)
    feature_ramp = jnp.exp(0.5 * jnp.log(3.0) * jnp.arange(MODEL_WIDTH, dtype=jnp.float32) / MODEL_WIDTH)
    sampled_batch = jax.random.normal(key, (STEPS, BATCH_ROW_COUNT, MODEL_WIDTH), jnp.float32) * feature_ramp
    return sampled_batch.astype(jnp.bfloat16)


def draw_cache_k(key, part):
    key = jax.random.fold_in(key, 12)
    sampled_batch = jax.random.normal(key, (BATCH_ROW_COUNT, CACHE_SLOTS, KEY_VALUE_HEADS * HEAD_SIZE), jnp.float32)
    return sampled_batch.astype(jnp.bfloat16)


def draw_lengths(key, part):
    key = jax.random.fold_in(key, 13)
    key_len, key_row = jax.random.split(key)
    drawn_len = jax.random.randint(key_len, (BATCH_ROW_COUNT,), 1, CACHE_SLOTS + 1)
    full_row = jax.random.randint(key_row, (), 0, BATCH_ROW_COUNT)
    return jnp.where(jnp.arange(BATCH_ROW_COUNT) == full_row, CACHE_SLOTS, drawn_len).astype(jnp.int32)


def draw_block_of_slot(key, part):
    key = jax.random.fold_in(key, 14)
    row_keys = jax.random.split(key, BATCH_ROW_COUNT)
    return jax.vmap(lambda row_key: jax.random.permutation(row_key, NBLK))(row_keys).astype(jnp.int32)


def shard_levels(own_key, dims, cuts, smallest, high):
    loudness, own = 1.0, jax.random.fold_in(own_key, 6)
    for position, shards_of in cuts:
        heights = jnp.exp(jax.random.uniform(jax.random.fold_in(own, position), (shards_of,), jnp.float32, smallest / len(cuts), high / len(cuts)))
        loudness = loudness * jnp.repeat(heights, dims[position] // shards_of).reshape([-1 if axis == position else 1 for axis in range(len(dims))])
    return loudness


def noise(own_key, shape, deviation, most, pieces=(), kind=jnp.bfloat16):
    drawn = deviation * jax.random.normal(own_key, shape, jnp.float32)
    if pieces:
        drawn = drawn * shard_levels(own_key, shape, pieces, -0.22, 0.18)
    return jnp.clip(drawn, -most, most).astype(kind)


def setup_inputs(seed: int = 0) -> dict:
    splits = jax.random.split(jax.random.key(seed), 27)
    return {
        "embeds": draw_embeds(jax.random.fold_in(splits[26], 71), 0),
        "norm_mamba": jnp.clip(1.0 + 0.18 * jax.random.normal(splits[1], (MODEL_WIDTH,), jnp.float32), 0.1, 1.9),
        "in_x": noise(splits[2], (MODEL_WIDTH, DI), MODEL_WIDTH ** -0.5, 0.0625, ((0, 32), (1, 8))),
        "in_z": noise(splits[3], (MODEL_WIDTH, DI), MODEL_WIDTH ** -0.5, 0.0625, ((0, 32), (1, 8))),
        "conv_w": noise(splits[4], (CONV, DI), 0.5, 3.0, ((1, 8),), jnp.float32),
        "conv_b": noise(splits[5], (DI,), 0.5, 3.0, ((0, 8),), jnp.float32),
        "x_proj": noise(splits[6], (DI, DTR + 2 * DS), DI ** -0.5, 0.046875, ((0, 8),)),
        "dt_norm": jnp.clip(1.0 + 0.18 * jax.random.normal(splits[7], (DTR,), jnp.float32), 0.1, 1.9),
        "b_norm": jnp.clip(1.0 + 0.18 * jax.random.normal(splits[8], (DS,), jnp.float32), 0.1, 1.9),
        "c_norm": jnp.clip(1.0 + 0.18 * jax.random.normal(splits[9], (DS,), jnp.float32), 0.1, 1.9),
        "dt_proj": noise(splits[10], (DTR, DI), DTR ** -0.5, 0.25, ((1, 8),)),
        "dt_bias": jnp.clip(-3.0 + 3.0 * jax.random.uniform(splits[11], (DI,), jnp.float32) ** shard_levels(splits[11], (DI,), ((0, 8),), -0.2, 0.2), -3.0, 0.0),
        "a_log": jnp.clip(2.77 * jax.random.uniform(splits[12], (DS, DI), jnp.float32) ** shard_levels(splits[12], (DS, DI), ((1, 8),), -0.2, 0.2), 0.0, 2.77),
        "d_skip": jnp.clip(0.5 + 1.0 * jax.random.uniform(splits[13], (DI,), jnp.float32) ** shard_levels(splits[13], (DI,), ((0, 8),), -0.2, 0.2), 0.5, 1.5),
        "out_proj": noise(splits[14], (DI, MODEL_WIDTH), DI ** -0.5, 0.046875, ((0, 8), (1, 32))),
        "norm_attn": jnp.clip(1.0 + 0.18 * jax.random.normal(splits[15], (MODEL_WIDTH,), jnp.float32), 0.1, 1.9),
        "w_query": noise(splits[16], (MODEL_WIDTH, QUERY_HEADS * HEAD_SIZE), MODEL_WIDTH ** -0.5, 0.0625, ((0, 32), (1, 8))),
        "key_matrix": noise(splits[17], (MODEL_WIDTH, KEY_VALUE_HEADS * HEAD_SIZE), MODEL_WIDTH ** -0.5, 0.0625, ((0, 32), (1, 8))),
        "value_matrix": noise(splits[18], (MODEL_WIDTH, KEY_VALUE_HEADS * HEAD_SIZE), MODEL_WIDTH ** -0.5, 0.0625, ((0, 32), (1, 8))),
        "w_out": noise(splits[19], (QUERY_HEADS * HEAD_SIZE, MODEL_WIDTH), (QUERY_HEADS * HEAD_SIZE) ** -0.5, 0.0625, ((0, 8), (1, 32))),
        "cache_k": draw_cache_k(jax.random.fold_in(splits[26], 71), 0),
        "value_cache": noise(splits[21], (BATCH_ROW_COUNT, CACHE_SLOTS, KEY_VALUE_HEADS * HEAD_SIZE), 1.0, 6.0, ((1, 32), (2, 8))),
        "lengths": draw_lengths(jax.random.fold_in(splits[26], 71), 0),
        "block_of_slot": draw_block_of_slot(jax.random.fold_in(splits[26], 71), 0),
        "conv_state": noise(splits[24], (BATCH_ROW_COUNT, CONV - 1, DI), 1.0, 6.0, ((2, 8),), jnp.float32),
        "ssm_state": noise(splits[25], (BATCH_ROW_COUNT, DS, DI), 1.0, 6.0, ((2, 8),), jnp.float32),
    }


def rms_scaled(values, gain):
    mean_sq = lax.optimization_barrier(jnp.mean(values * values, axis=-1, keepdims=True))
    return (values * lax.rsqrt(mean_sq + 1e-06) * gain).astype(jnp.bfloat16)

def rms_float(values, gain):
    mean_sq = lax.optimization_barrier(jnp.mean(values * values, axis=-1, keepdims=True))
    return values * lax.rsqrt(mean_sq + 1e-06) * gain

def attend_row(operands):
    row_query, row_key_list, row_value_list, live_row, incoming_keys, incoming_values = operands
    query_group_width = QUERY_HEADS // KEY_VALUE_HEADS
    query_head_list = row_query.reshape(KEY_VALUE_HEADS, query_group_width, HEAD_SIZE).astype(jnp.float32)
    every_key = jnp.concatenate([row_key_list, incoming_keys], axis=0).reshape(-1, KEY_VALUE_HEADS, HEAD_SIZE).astype(jnp.float32)
    every_value = jnp.concatenate([row_value_list, incoming_values], axis=0).reshape(-1, KEY_VALUE_HEADS, HEAD_SIZE).astype(jnp.float32)
    mask_all = jnp.concatenate([live_row, jnp.ones((incoming_keys.shape[0],), dtype=bool)])
    scores = jnp.einsum('kgd,skd->kgs', query_head_list, every_key) * (1.0 / jnp.sqrt(jnp.float32(HEAD_SIZE)))
    scores = jnp.where(mask_all, scores, jnp.float32(-1e+30))
    peak_score = lax.optimization_barrier(jnp.max(scores, axis=-1, keepdims=True))
    weights = jnp.where(mask_all, jnp.exp(scores - peak_score), jnp.float32(0.0))
    weight_sum = lax.optimization_barrier(jnp.sum(weights, axis=-1, keepdims=True))
    rounded = lax.optimization_barrier(weights.astype(jnp.bfloat16)).astype(jnp.float32)
    summed = jnp.einsum('kgs,skd->kgd', rounded, every_value)
    return (summed / weight_sum).reshape(QUERY_HEADS * HEAD_SIZE).astype(jnp.bfloat16)

def reference(embeds, norm_mamba, in_x, in_z, conv_w, conv_b, x_proj, dt_norm, b_norm, c_norm, dt_proj, dt_bias, a_log, d_skip, out_proj, norm_attn, w_query, key_matrix, value_matrix, w_out, cache_k, value_cache, lengths, block_of_slot, conv_state, ssm_state):
    decay_rate = -jnp.exp(a_log)
    offsets = jnp.arange(BLK, dtype=jnp.int32)
    positions = (block_of_slot[:, :, None] * BLK + offsets[None, None, :]).reshape(BATCH_ROW_COUNT, CACHE_SLOTS)
    live_slots = positions < lengths[:, None]
    conv_hist = conv_state
    state_now = ssm_state
    hidden_list, key_list, value_list = ([], [], [])
    for step_index in range(STEPS):
        residual = embeds[step_index].astype(jnp.float32)
        normed = rms_scaled(residual, norm_mamba)
        inner_x = jnp.dot(normed, in_x, preferred_element_type=jnp.float32)
        inner_z = jnp.dot(normed, in_z, preferred_element_type=jnp.float32)
        window = jnp.concatenate([conv_hist, inner_x[:, None, :]], axis=1)
        conv_hist = window[:, 1:, :]
        conv_mixed = jax.nn.silu(lax.optimization_barrier(jnp.sum(window * conv_w[None], axis=1)) + conv_b)
        low_rank = jnp.dot(conv_mixed.astype(jnp.bfloat16), x_proj, preferred_element_type=jnp.float32)
        dt_low = rms_scaled(low_rank[:, :DTR], dt_norm)
        b_in = rms_float(low_rank[:, DTR:DTR + DS], b_norm)
        c_out = rms_float(low_rank[:, DTR + DS:], c_norm)
        step_size = jax.nn.softplus(jnp.dot(dt_low, dt_proj, preferred_element_type=jnp.float32) + dt_bias)
        state_now = jnp.exp(step_size[:, None, :] * decay_rate[None]) * state_now + (step_size * conv_mixed)[:, None, :] * b_in[:, :, None]
        mamba_y = lax.optimization_barrier(jnp.sum(c_out[:, :, None] * state_now, axis=1)) + d_skip * conv_mixed
        mamba_y = (mamba_y * jax.nn.silu(inner_z)).astype(jnp.bfloat16)
        residual = residual + jnp.dot(mamba_y, out_proj, preferred_element_type=jnp.float32)
        normed2 = rms_scaled(residual, norm_attn)
        query_now = jnp.dot(normed2, w_query, preferred_element_type=jnp.float32).astype(jnp.bfloat16)
        key_now = jnp.dot(normed2, key_matrix, preferred_element_type=jnp.float32).astype(jnp.bfloat16)
        value_now = jnp.dot(normed2, value_matrix, preferred_element_type=jnp.float32).astype(jnp.bfloat16)
        key_list.append(key_now)
        value_list.append(value_now)
        incoming_keys = jnp.stack(key_list, axis=1)
        incoming_values = jnp.stack(value_list, axis=1)
        attended = lax.map(attend_row, (query_now, cache_k, value_cache, live_slots, incoming_keys, incoming_values))
        residual = residual + jnp.dot(attended, w_out, preferred_element_type=jnp.float32)
        hidden_list.append(residual)
    return (jnp.stack(hidden_list), jnp.stack(key_list), jnp.stack(value_list), state_now, conv_hist)
```

```python
import jax
import jax.numpy as jnp
from jax import lax
from jax.sharding import Mesh, PartitionSpec as P

DS = 16
DTR = 512
HEAD_SIZE = 128
BLK = 128
STEPS = 3
ROWS = 8
ALL_ROWS = STEPS * ROWS
X_SIZE = 4
CTX = ("z", "x")
bf16 = jnp.bfloat16
f32 = jnp.float32


def split_two(value):
    hi = value.astype(bf16)
    return hi, (value - hi.astype(f32)).astype(bf16)


def split_three(value):
    hi = value.astype(bf16)
    rest = value - hi.astype(f32)
    mid = rest.astype(bf16)
    return hi, mid, (rest - mid.astype(f32)).astype(bf16)


def exchange(parts, axis):
    return lax.all_to_all(parts, axis, 0, 0, tiled=True)


def share(part, axis):
    return exchange(jnp.broadcast_to(part[None], (lax.axis_size(axis),) + part.shape), axis)


def sum_over(part, axis):
    return jnp.sum(share(part.astype(bf16), axis).astype(f32), axis=0)


def rms_float(values, gain):
    mean_sq = jnp.mean(values * values, axis=-1, keepdims=True)
    return values * lax.rsqrt(mean_sq + 1e-06) * gain


def stat_rows(stats, width):
    return jnp.stack([jnp.pad(stat, (0, width - stat.shape[0])) for stat in stats])


def body(
    embeds, norm_mamba, in_x, in_z, conv_w, conv_b, x_proj, dt_norm, b_norm, c_norm, dt_proj,
    dt_bias, a_log, d_skip, out_proj, norm_attn, w_query, key_matrix, value_matrix, w_out,
    cache_k, value_cache, lengths, block_of_slot, conv_state, ssm_state,
):
    ctx_size = lax.axis_size(CTX)
    local_width = embeds.shape[2]
    width_all = local_width * ctx_size
    channels = in_x.shape[1]
    slots = cache_k.shape[1]
    heads = w_query.shape[1] // HEAD_SIZE

    rows_in = embeds.reshape(ALL_ROWS, local_width).astype(f32)
    squares = jnp.sum(rows_in * rows_in, axis=-1)
    scaled = (rows_in * norm_mamba).astype(bf16)
    part_x = jnp.dot(scaled, in_x, preferred_element_type=f32)
    part_z = jnp.dot(scaled, in_z, preferred_element_type=f32)
    chunk = 2 * channels // ctx_size
    chunks = jnp.concatenate(
        [
            part.astype(bf16).reshape(ALL_ROWS, channels // chunk, chunk).transpose(1, 0, 2)
            for part in (part_x, part_z)
        ],
        axis=0,
    )
    stats = stat_rows(split_two(squares), chunk)
    chunks = jnp.concatenate(
        [chunks, jnp.broadcast_to(stats[None], (ctx_size, 2, chunk))], axis=1
    )
    summed = jnp.sum(exchange(chunks, CTX).astype(f32), axis=0)
    mean_sq = (summed[ALL_ROWS, :ALL_ROWS] + summed[ALL_ROWS + 1, :ALL_ROWS]) / width_all
    mine = summed[:ALL_ROWS] * lax.rsqrt(mean_sq + 1e-06)[:, None]
    inner = share(mine.astype(bf16), CTX)
    inner = inner.astype(f32).transpose(1, 0, 2).reshape(ALL_ROWS, 2 * channels)
    inner_x = inner[:, :channels].reshape(STEPS, ROWS, channels)
    inner_z = inner[:, channels:]

    history = jnp.concatenate([conv_state.transpose(1, 0, 2), inner_x], axis=0)
    conv_out = history[STEPS:].transpose(1, 0, 2)
    mixed = sum(history[tap : tap + STEPS] * conv_w[tap][None, None] for tap in range(4))
    mixed = jax.nn.silu(mixed + conv_b).reshape(ALL_ROWS, channels)
    low_part = jnp.dot(mixed.astype(bf16), x_proj, preferred_element_type=f32)
    low_rank = sum_over(low_part, "tp")
    dt_low = rms_float(low_rank[:, :DTR], dt_norm).astype(bf16)
    b_in = rms_float(low_rank[:, DTR : DTR + DS], b_norm).reshape(STEPS, ROWS, DS)
    c_out = rms_float(low_rank[:, DTR + DS :], c_norm).reshape(STEPS, ROWS, DS)
    step_size = jax.nn.softplus(
        jnp.dot(dt_low, dt_proj, preferred_element_type=f32) + dt_bias
    ).reshape(STEPS, ROWS, channels)
    decay_rate = -jnp.exp(a_log)
    mixed = mixed.reshape(STEPS, ROWS, channels)
    state = ssm_state
    scanned = []
    for step in range(STEPS):
        state = (
            jnp.exp(step_size[step][:, None, :] * decay_rate[None]) * state
            + (step_size[step] * mixed[step])[:, None, :] * b_in[step][:, :, None]
        )
        scanned.append(
            jnp.sum(c_out[step][:, :, None] * state, axis=1) + d_skip * mixed[step]
        )
    mamba_y = (jnp.concatenate(scanned, axis=0) * jax.nn.silu(inner_z)).astype(bf16)
    mamba_part = jnp.dot(mamba_y, out_proj, preferred_element_type=f32)
    residual = rows_in + sum_over(mamba_part, "tp")

    squares = jnp.sum(residual * residual, axis=-1)
    scaled = (residual * norm_attn).astype(bf16)
    projected = jnp.concatenate(
        [
            jnp.dot(scaled, weight, preferred_element_type=f32)
            for weight in (w_query, key_matrix, value_matrix)
        ],
        axis=1,
    )
    projected = jnp.concatenate(
        [
            projected,
            jnp.pad(squares[:, None], ((0, 0), (0, HEAD_SIZE - 1))),
        ],
        axis=1,
    )
    hi, lo = split_two(projected[:, -HEAD_SIZE])
    projected = projected.astype(bf16)
    projected = projected.at[:, -HEAD_SIZE].set(hi).at[:, 1 - HEAD_SIZE].set(lo)
    over_x = jnp.sum(share(projected, "x").astype(f32), axis=0)
    hi, lo = split_two(over_x[:, -HEAD_SIZE] + over_x[:, 1 - HEAD_SIZE])
    over_x = over_x.astype(bf16).at[:, -HEAD_SIZE].set(hi).at[:, 1 - HEAD_SIZE].set(lo)
    over_all = jnp.sum(share(over_x, "z").astype(f32), axis=0)
    mean_sq = (over_all[:, -HEAD_SIZE] + over_all[:, 1 - HEAD_SIZE]) / width_all
    over_all = (over_all * lax.rsqrt(mean_sq + 1e-06)[:, None]).astype(bf16)
    query = over_all[:, : heads * HEAD_SIZE]
    new_keys = over_all[:, heads * HEAD_SIZE : (heads + 1) * HEAD_SIZE]
    new_values = over_all[:, (heads + 1) * HEAD_SIZE : (heads + 2) * HEAD_SIZE]
    new_keys = new_keys.reshape(STEPS, ROWS, HEAD_SIZE)
    new_values = new_values.reshape(STEPS, ROWS, HEAD_SIZE)

    query = (
        query.reshape(STEPS, ROWS, heads, HEAD_SIZE)
        .transpose(1, 0, 2, 3)
        .reshape(ROWS, STEPS * heads, HEAD_SIZE)
    )
    negative = f32(-1e30)
    score_scale = 1.0 / jnp.sqrt(f32(HEAD_SIZE))
    offsets = jnp.arange(BLK, dtype=jnp.int32)
    positions = (block_of_slot[:, :, None] * BLK + offsets[None, None, :]).reshape(ROWS, slots)
    live = (positions < lengths[:, None])[:, None, :]
    scores = jnp.einsum("rqd,rsd->rqs", query, cache_k, preferred_element_type=f32) * score_scale
    scores = jnp.where(live, scores, negative)
    fresh = (
        jnp.einsum("rqd,trd->rqt", query, new_keys, preferred_element_type=f32) * score_scale
    )
    step_of_query = jnp.arange(STEPS * heads) // heads
    fresh_live = (jnp.arange(STEPS)[None, :] <= step_of_query[:, None])[None]
    fresh_live = fresh_live & (lax.axis_index(CTX) == 0)
    fresh = jnp.where(fresh_live, fresh, negative)
    peak = jnp.maximum(jnp.max(scores, axis=-1), jnp.max(fresh, axis=-1))[..., None]
    weights = jnp.where(live, jnp.exp(scores - peak), 0.0)
    fresh_weights = jnp.where(fresh_live, jnp.exp(fresh - peak), 0.0)
    total = jnp.sum(weights, axis=-1) + jnp.sum(fresh_weights, axis=-1)
    attended = jnp.einsum(
        "rqs,rsd->rqd", weights.astype(bf16), value_cache, preferred_element_type=f32
    ) + jnp.einsum(
        "rqt,trd->rqd", fresh_weights.astype(bf16), new_values, preferred_element_type=f32
    )
    safe_total = jnp.where(total > 0, total, 1.0)
    attended = attended / safe_total[..., None]
    log_sum = jnp.where(total > 0, peak[..., 0] + jnp.log(safe_total), negative)

    def combine(attended, log_sum, axis):
        stats = jnp.stack(split_three(log_sum), axis=1)
        stats = jnp.pad(stats, ((0, 0), (0, 0), (0, HEAD_SIZE - stats.shape[2])))
        both = share(jnp.concatenate([attended.astype(bf16), stats], axis=1), axis).astype(f32)
        queries = attended.shape[1]
        logs = both[:, :, queries, :queries]
        logs = logs + both[:, :, queries + 1, :queries] + both[:, :, queries + 2, :queries]
        top = jnp.max(logs, axis=0)
        shares = jnp.exp(logs - top[None])
        total = jnp.sum(shares, axis=0)
        attended = jnp.sum(both[:, :, :queries] * shares[..., None], axis=0) / total[..., None]
        return attended, top + jnp.log(total)

    attended, log_sum = combine(attended, log_sum, "x")
    attended, log_sum = combine(attended, log_sum, "z")
    attended = (
        attended.astype(bf16)
        .reshape(ROWS, STEPS, heads, HEAD_SIZE)
        .transpose(1, 0, 2, 3)
        .reshape(ALL_ROWS, heads * HEAD_SIZE)
    )
    attn_part = jnp.dot(attended, w_out, preferred_element_type=f32)
    hidden = residual + sum_over(attn_part, "tp")
    return (
        hidden.reshape(STEPS, ROWS, local_width),
        new_keys,
        new_values,
        state,
        conv_out,
    )


def solution(mesh):
    ctx_size, tp_size = mesh.devices.shape
    split = Mesh(
        mesh.devices.reshape(ctx_size // X_SIZE, X_SIZE, tp_size), ("z", "x", "tp")
    )
    return jax.shard_map(
        body,
        mesh=split,
        in_specs=(
            P(None, None, CTX),
            P(CTX),
            P(CTX, "tp"),
            P(CTX, "tp"),
            P(None, "tp"),
            P("tp"),
            P("tp", None),
            P(),
            P(),
            P(),
            P(None, "tp"),
            P("tp"),
            P(None, "tp"),
            P("tp"),
            P("tp", CTX),
            P(CTX),
            P(CTX, "tp"),
            P(CTX, "tp"),
            P(CTX, "tp"),
            P("tp", CTX),
            P(None, CTX, "tp"),
            P(None, CTX, "tp"),
            P(),
            P(None, CTX),
            P(None, None, "tp"),
            P(None, None, "tp"),
        ),
        out_specs=(
            P(None, None, CTX),
            P(None, None, "tp"),
            P(None, None, "tp"),
            P(None, None, "tp"),
            P(None, None, "tp"),
        ),
        check_vma=False,
    )
```

```python
import functools

import jax
import jax.numpy as jnp
from jax import lax
from jax.experimental import pallas as pl
from jax.experimental.pallas import tpu as pltpu
from jax.sharding import Mesh, PartitionSpec as P

DS = 16
DTR = 512
HEAD = 128
BLK = 128
STEPS = 3
ROWS = 8
ALL_ROWS = STEPS * ROWS
LANES = 128
X_SIZE = 4
CTX = ("z", "x")
NEGATIVE = -1e30
bf16 = jnp.bfloat16
f32 = jnp.float32


def exchange(parts, axis):
    return lax.all_to_all(parts, axis, 0, 0, tiled=True)


def from_partners(part):
    received = {
        flip: lax.ppermute(part, "x", [(i, i ^ flip) for i in range(X_SIZE)])
        for flip in (1, 3, 2)
    }
    return received[1], received[2], received[3]


def call(kernel, outs, *operands, **options):
    return pl.pallas_call(
        kernel,
        out_shape=[jax.ShapeDtypeStruct(shape, dtype) for shape, dtype in outs],
        compiler_params=pltpu.CompilerParams(vmem_limit_bytes=48 * 1024 * 1024),
        **options,
    )(*operands)


def lane_index(rows, lanes=LANES):
    return lax.broadcasted_iota(jnp.int32, (rows, lanes), 1)


def row_index(rows, lanes=LANES):
    return lax.broadcasted_iota(jnp.int32, (rows, lanes), 0)


def rounded(value):
    return value.astype(bf16).astype(f32)


def silu(value):
    return value / (1.0 + jnp.exp(-value))


def project_kernel(rows_ref, gain_ref, wx_ref, wz_ref, out_ref):
    rows = rows_ref[...].astype(f32)
    scaled = (rows * gain_ref[...]).astype(bf16)
    column = jnp.sum(rows * rows, axis=1, keepdims=True)
    eye = row_index(ALL_ROWS) == lane_index(ALL_ROWS)
    squares = jnp.sum(jnp.where(eye, column, 0.0), axis=0, keepdims=True)
    hi = rounded(squares)
    which = row_index(8)
    stats = jnp.where(which == 0, hi, jnp.where(which == 1, squares - hi, 0.0))
    for half, weight_ref in enumerate((wx_ref, wz_ref)):
        part = jnp.dot(scaled, weight_ref[...], preferred_element_type=f32)
        for k in range(out_ref.shape[1]):
            chunk = part[:, k * LANES : (k + 1) * LANES]
            out_ref[half, k] = jnp.concatenate([chunk, stats], axis=0).astype(bf16)


def reduce_kernel(width_all, in_ref, out_ref):
    total = in_ref[0].astype(f32)
    for source in range(1, in_ref.shape[0]):
        total = total + in_ref[source].astype(f32)
    squares = total[ALL_ROWS : ALL_ROWS + 1] + total[ALL_ROWS + 1 : ALL_ROWS + 2]
    eye = row_index(ALL_ROWS) == lane_index(ALL_ROWS)
    column = jnp.sum(jnp.where(eye, squares, 0.0), axis=1, keepdims=True)
    mine = (total[:ALL_ROWS] * lax.rsqrt(column / width_all + 1e-06)).astype(bf16)
    for target in range(out_ref.shape[0]):
        out_ref[target] = mine


def conv_kernel(inner_ref, hist_ref, taps_ref, bias_ref, xp_ref, low_ref, mixed_ref, hist_out_ref, mixed16):
    for k in range(mixed_ref.shape[1] // LANES):
        cols = slice(k * LANES, (k + 1) * LANES)
        fresh = inner_ref[k].astype(f32)
        window = [hist_ref[t, :, cols] for t in range(STEPS)]
        window += [fresh[s * ROWS : (s + 1) * ROWS] for s in range(STEPS)]
        taps = taps_ref[:, cols]
        bias = bias_ref[:, cols]
        mixed = []
        for s in range(STEPS):
            total = window[s] * taps[0:1]
            for t in range(1, STEPS + 1):
                total = total + window[s + t] * taps[t : t + 1]
            mixed.append(silu(total + bias))
            hist_out_ref[s, :, cols] = window[STEPS + s]
        mixed = jnp.concatenate(mixed, axis=0)
        mixed_ref[:, cols] = mixed
        mixed16[:, cols] = mixed.astype(bf16)
    low = jnp.dot(mixed16[...], xp_ref[...], preferred_element_type=f32).astype(bf16)
    for target in range(low_ref.shape[0]):
        low_ref[target] = low


def scan_kernel(
    low_ref, dt_gain_ref, bc_gain_ref, dtp_ref, dt_bias_ref, a_ref, skip_ref, mixed_ref,
    gate_ref, state_ref, op_ref, state_out_ref, part_ref, dt16, b_wide, c_wide, y_rows, total,
):
    step_index = pl.program_id(0)

    @pl.when(step_index == 0)
    def _():
        low = low_ref[0].astype(f32)
        for source in range(1, low_ref.shape[0]):
            low = low + low_ref[source].astype(f32)
        raw = low[:, :DTR]
        mean_sq = jnp.sum(raw * raw, axis=1, keepdims=True) / DTR
        dt16[...] = (raw * lax.rsqrt(mean_sq + 1e-06) * dt_gain_ref[...]).astype(bf16)
        raw = low[:, DTR:]
        is_b = lane_index(ALL_ROWS, 2 * DS) < DS
        squares = raw * raw
        mean_b = jnp.sum(jnp.where(is_b, squares, 0.0), axis=1, keepdims=True) / DS
        mean_c = jnp.sum(jnp.where(is_b, 0.0, squares), axis=1, keepdims=True) / DS
        scale = jnp.where(is_b, lax.rsqrt(mean_b + 1e-06), lax.rsqrt(mean_c + 1e-06))
        normed = raw * scale * bc_gain_ref[...]
        eye_b = lane_index(DS, 2 * DS) == row_index(DS, 2 * DS)
        eye_c = lane_index(DS, 2 * DS) == row_index(DS, 2 * DS) + DS
        for r in range(ALL_ROWS):
            row = normed[r : r + 1]
            for eye, wide in ((eye_b, b_wide), (eye_c, c_wide)):
                column = jnp.sum(jnp.where(eye, row, 0.0), axis=1, keepdims=True)
                wide[r] = jnp.broadcast_to(column, (DS, LANES))
        total[...] = jnp.zeros_like(total)

    raw = jnp.dot(dt16[...], dtp_ref[...], preferred_element_type=f32) + dt_bias_ref[...]
    steps = jnp.maximum(raw, 0.0) + jnp.log1p(jnp.exp(-jnp.abs(raw)))
    mixed = mixed_ref[...]
    drive = steps * mixed
    width = mixed.shape[1]
    for k in range(width // LANES):
        cols = slice(k * LANES, (k + 1) * LANES)
        decay = -jnp.exp(a_ref[:, cols])
        for b in range(ROWS):
            state = state_ref[b, :, cols]
            for s in range(STEPS):
                r = s * ROWS + b
                state = (
                    jnp.exp(steps[r : r + 1, cols] * decay) * state
                    + drive[r : r + 1, cols] * b_wide[r]
                )
                y_rows[r : r + 1, cols] = jnp.sum(c_wide[r] * state, axis=0, keepdims=True)
            state_out_ref[b, :, cols] = state
    gate = jnp.concatenate(
        [gate_ref[k].astype(f32) for k in range(width // LANES)], axis=1
    )
    y = ((y_rows[...] + skip_ref[...] * mixed) * silu(gate)).astype(bf16)
    total[...] += jnp.dot(y, op_ref[...], preferred_element_type=f32)

    @pl.when(step_index == pl.num_programs(0) - 1)
    def _():
        part = total[...].astype(bf16)
        for target in range(part_ref.shape[0]):
            part_ref[target] = part


def qkv_kernel(parts_ref, rows_ref, gain_ref, wq_ref, wk_ref, wv_ref, residual_ref, out_ref):
    total = parts_ref[0].astype(f32)
    for source in range(1, parts_ref.shape[0]):
        total = total + parts_ref[source].astype(f32)
    residual = rows_ref[...].astype(f32) + total
    residual_ref[...] = residual
    scaled = (residual * gain_ref[...]).astype(bf16)
    column = jnp.sum(residual * residual, axis=1, keepdims=True)
    at = 0
    for weight_ref in (wq_ref, wk_ref, wv_ref):
        width = weight_ref.shape[1]
        out_ref[:, at : at + width] = jnp.dot(
            scaled, weight_ref[...], preferred_element_type=f32
        ).astype(bf16)
        at += width
    out_ref[:, at:] = pair_columns(column).astype(bf16)


def pair_columns(column):
    hi = rounded(column)
    which = lane_index(ALL_ROWS)
    return jnp.where(which == 0, hi, jnp.where(which == 1, column - hi, 0.0))


def qkv_sum_kernel(own_ref, one_ref, two_ref, three_ref, out_ref):
    total = (own_ref[...].astype(f32) + one_ref[...].astype(f32)) + (
        two_ref[...].astype(f32) + three_ref[...].astype(f32)
    )
    column = jnp.sum(total[:, -LANES:], axis=1, keepdims=True)
    body = total[:, :-LANES].astype(bf16)
    last = pair_columns(column).astype(bf16)
    for target in range(out_ref.shape[0]):
        out_ref[target, :, :-LANES] = body
        out_ref[target, :, -LANES:] = last


def pack_logs(logs):
    which = lane_index(ALL_ROWS)
    logs = jnp.where(which < ROWS, logs, 0.0)
    hi = rounded(logs)
    mid = rounded(logs - hi)
    low = logs - hi - mid
    return hi + pltpu.roll(mid, ROWS, 1) + pltpu.roll(low, 2 * ROWS, 1)


def unpack_logs(packed):
    return (
        packed + pltpu.roll(packed, LANES - ROWS, 1) + pltpu.roll(packed, LANES - 2 * ROWS, 1)
    )


def attention_kernel(
    width_all, first_ref, parts_ref, live_ref, keys_ref, values_ref,
    new_keys_ref, new_values_ref, out_ref, query, fresh_k, fresh_v,
):
    total = parts_ref[0].astype(f32)
    for source in range(1, parts_ref.shape[0]):
        total = total + parts_ref[source].astype(f32)
    column = jnp.sum(total[:, -LANES:], axis=1, keepdims=True)
    total = rounded(total[:, :-LANES] * lax.rsqrt(column / width_all + 1e-06))
    heads = total.shape[1] // HEAD - 2
    keys_now = total[:, heads * HEAD : (heads + 1) * HEAD]
    values_now = total[:, (heads + 1) * HEAD :]
    new_keys_ref[...] = keys_now.astype(bf16)
    new_values_ref[...] = values_now.astype(bf16)
    fresh_k[...] = jnp.zeros_like(fresh_k)
    fresh_v[...] = jnp.zeros_like(fresh_v)
    for s in range(STEPS):
        rows = slice(s * ROWS, (s + 1) * ROWS)
        fresh_k[:, s, :] = keys_now[rows]
        fresh_v[:, s, :] = values_now[rows]
        for g in range(heads):
            query[:, s * heads + g, :] = total[rows, g * HEAD : (g + 1) * HEAD]
    queries = STEPS * heads
    which = lane_index(queries, ROWS)
    fresh_live = (which * heads <= row_index(queries, ROWS)) & (which < STEPS)
    fresh_live = fresh_live & (first_ref[0] == 1)
    score_scale = HEAD**-0.5
    lanes = lane_index(queries)
    logs = jnp.zeros((queries, LANES), f32)
    contract = (((1,), (1,)), ((), ()))
    for b in range(ROWS):
        query_b = query[b].astype(bf16)
        live = jnp.broadcast_to(live_ref[b : b + 1, :], (queries, live_ref.shape[1])) > 0
        scores = lax.dot_general(query_b, keys_ref[b], contract, preferred_element_type=f32)
        scores = jnp.where(live, scores * score_scale, NEGATIVE)
        fresh = lax.dot_general(
            query_b, fresh_k[b].astype(bf16), contract, preferred_element_type=f32
        )
        fresh = jnp.where(fresh_live, fresh * score_scale, NEGATIVE)
        peak = jnp.maximum(
            jnp.max(scores, axis=1, keepdims=True), jnp.max(fresh, axis=1, keepdims=True)
        )
        weights = jnp.where(live, jnp.exp(scores - peak), 0.0)
        fresh_weights = jnp.where(fresh_live, jnp.exp(fresh - peak), 0.0)
        weight_sum = jnp.sum(weights, axis=1, keepdims=True) + jnp.sum(
            fresh_weights, axis=1, keepdims=True
        )
        attended = jnp.dot(weights.astype(bf16), values_ref[b], preferred_element_type=f32)
        attended = attended + jnp.dot(
            fresh_weights.astype(bf16), fresh_v[b].astype(bf16), preferred_element_type=f32
        )
        any_live = weight_sum > 0
        safe = jnp.where(any_live, weight_sum, 1.0)
        out_ref[b] = (attended / safe).astype(bf16)
        log_sum = jnp.where(any_live, peak + jnp.log(safe), NEGATIVE)
        logs = jnp.where(lanes == b, log_sum, logs)
    out_ref[ROWS] = pack_logs(logs).astype(bf16)


def shares_of(refs):
    logs = [unpack_logs(ref[ROWS].astype(f32)) for ref in refs]
    top = functools.reduce(jnp.maximum, logs)
    shares = [jnp.exp(log - top) for log in logs]
    total = functools.reduce(jnp.add, shares)
    return [share / total for share in shares], top + jnp.log(total)


def combined_row(refs, shares, b):
    attended = [shares[i][:, b : b + 1] * ref[b].astype(f32) for i, ref in enumerate(refs)]
    return functools.reduce(jnp.add, attended)


def combine_x_kernel(own_ref, one_ref, two_ref, three_ref, out_ref):
    refs = (own_ref, one_ref, two_ref, three_ref)
    shares, logs = shares_of(refs)
    packed = pack_logs(logs).astype(bf16)
    for b in range(ROWS):
        attended = combined_row(refs, shares, b).astype(bf16)
        for target in range(out_ref.shape[0]):
            out_ref[target, b] = attended
    for target in range(out_ref.shape[0]):
        out_ref[target, ROWS] = packed


def combine_z_kernel(parts_ref, weight_ref, out_ref, attended):
    refs = [parts_ref.at[source] for source in range(parts_ref.shape[0])]
    shares, _ = shares_of(refs)
    for b in range(ROWS):
        attended[b] = combined_row(refs, shares, b)
    heads = attended.shape[1] // STEPS
    rows = jnp.concatenate(
        [
            jnp.concatenate([attended[:, s * heads + g, :] for g in range(heads)], axis=1)
            for s in range(STEPS)
        ],
        axis=0,
    ).astype(bf16)
    part = jnp.dot(rows, weight_ref[...], preferred_element_type=f32).astype(bf16)
    for target in range(out_ref.shape[0]):
        out_ref[target] = part


def body(
    embeds, norm_mamba, in_x, in_z, conv_w, conv_b, x_proj, dt_norm, b_norm, c_norm, dt_proj,
    dt_bias, a_log, d_skip, out_proj, norm_attn, w_query, key_matrix, value_matrix, w_out,
    cache_k, value_cache, lengths, block_of_slot, conv_state, ssm_state,
):
    ctx_size, z_size, tp_size = (lax.axis_size(axis) for axis in (CTX, "z", "tp"))
    local_width = embeds.shape[2]
    width_all = float(local_width * ctx_size)
    channels = in_x.shape[1]
    slots = cache_k.shape[1]
    heads = w_query.shape[1] // HEAD
    queries = STEPS * heads
    chunk_count = channels // LANES
    rows_in = embeds.reshape(ALL_ROWS, local_width)

    grid = 4
    per = chunk_count // grid
    cols = per * LANES
    (chunks,) = call(
        project_kernel,
        [((2, chunk_count, 32, LANES), bf16)],
        rows_in,
        norm_mamba.reshape(1, -1),
        in_x,
        in_z,
        grid=(grid,),
        in_specs=[
            pl.BlockSpec((ALL_ROWS, local_width), lambda i: (0, 0)),
            pl.BlockSpec((1, local_width), lambda i: (0, 0)),
            pl.BlockSpec((local_width, cols), lambda i: (0, i)),
            pl.BlockSpec((local_width, cols), lambda i: (0, i)),
        ],
        out_specs=[pl.BlockSpec((2, per, 32, LANES), lambda i: (0, i, 0, 0))],
    )
    received = exchange(chunks.reshape(2 * chunk_count, 32, LANES), CTX)
    (mine,) = call(
        functools.partial(reduce_kernel, width_all),
        [((ctx_size, ALL_ROWS, LANES), bf16)],
        received,
    )
    inner = exchange(mine, CTX)

    low, mixed, history = call(
        conv_kernel,
        [
            ((tp_size, ALL_ROWS, DTR + 2 * DS), bf16),
            ((ALL_ROWS, channels), f32),
            ((STEPS, ROWS, channels), f32),
        ],
        inner,
        conv_state.transpose(1, 0, 2),
        conv_w,
        conv_b.reshape(1, -1),
        x_proj,
        scratch_shapes=[pltpu.VMEM((ALL_ROWS, channels), bf16)],
    )
    low = exchange(low, "tp")
    state, part = call(
        scan_kernel,
        [(ssm_state.shape, f32), ((tp_size, ALL_ROWS, local_width), bf16)],
        low,
        dt_norm.reshape(1, -1),
        jnp.concatenate([b_norm, c_norm]).reshape(1, -1),
        dt_proj,
        dt_bias.reshape(1, -1),
        a_log,
        d_skip.reshape(1, -1),
        mixed,
        inner,
        ssm_state,
        out_proj,
        grid=(grid,),
        in_specs=[
            pl.BlockSpec(low.shape, lambda i: (0, 0, 0)),
            pl.BlockSpec((1, DTR), lambda i: (0, 0)),
            pl.BlockSpec((1, 2 * DS), lambda i: (0, 0)),
            pl.BlockSpec((DTR, cols), lambda i: (0, i)),
            pl.BlockSpec((1, cols), lambda i: (0, i)),
            pl.BlockSpec((DS, cols), lambda i: (0, i)),
            pl.BlockSpec((1, cols), lambda i: (0, i)),
            pl.BlockSpec((ALL_ROWS, cols), lambda i: (0, i)),
            pl.BlockSpec((per, ALL_ROWS, LANES), lambda i: (grid + i, 0, 0)),
            pl.BlockSpec((ROWS, DS, cols), lambda i: (0, 0, i)),
            pl.BlockSpec((cols, local_width), lambda i: (i, 0)),
        ],
        out_specs=[
            pl.BlockSpec((ROWS, DS, cols), lambda i: (0, 0, i)),
            pl.BlockSpec((tp_size, ALL_ROWS, local_width), lambda i: (0, 0, 0)),
        ],
        scratch_shapes=[
            pltpu.VMEM((ALL_ROWS, DTR), bf16),
            pltpu.VMEM((ALL_ROWS, DS, LANES), f32),
            pltpu.VMEM((ALL_ROWS, DS, LANES), f32),
            pltpu.VMEM((ALL_ROWS, cols), f32),
            pltpu.VMEM((ALL_ROWS, local_width), f32),
        ],
    )
    part = exchange(part, "tp")

    packed_width = (heads + 3) * HEAD
    residual, projected = call(
        qkv_kernel,
        [((ALL_ROWS, local_width), f32), ((ALL_ROWS, packed_width), bf16)],
        part,
        rows_in,
        norm_attn.reshape(1, -1),
        w_query,
        key_matrix,
        value_matrix,
    )
    (projected,) = call(
        qkv_sum_kernel,
        [((z_size, ALL_ROWS, packed_width), bf16)],
        projected,
        *from_partners(projected),
    )
    projected = exchange(projected, "z")

    offsets = jnp.arange(BLK, dtype=jnp.int32)
    positions = (block_of_slot[:, :, None] * BLK + offsets[None, None, :]).reshape(ROWS, slots)
    live = (positions < lengths[:, None]).astype(f32)
    first = (lax.axis_index(CTX) == 0).astype(jnp.int32).reshape(1)
    vmem = pl.BlockSpec(memory_space=pltpu.VMEM)
    new_keys, new_values, attended = call(
        functools.partial(attention_kernel, width_all),
        [
            ((ALL_ROWS, HEAD), bf16),
            ((ALL_ROWS, HEAD), bf16),
            ((ROWS + 1, queries, HEAD), bf16),
        ],
        first,
        projected,
        live,
        cache_k,
        value_cache,
        in_specs=[pl.BlockSpec(memory_space=pltpu.SMEM)] + [vmem] * 4,
        scratch_shapes=[
            pltpu.VMEM((ROWS, queries, HEAD), f32),
            pltpu.VMEM((ROWS, 8, HEAD), f32),
            pltpu.VMEM((ROWS, 8, HEAD), f32),
        ],
    )
    (attended,) = call(
        combine_x_kernel,
        [((z_size,) + attended.shape, bf16)],
        attended,
        *from_partners(attended),
    )
    attended = exchange(attended, "z")
    (part,) = call(
        combine_z_kernel,
        [((tp_size, ALL_ROWS, local_width), bf16)],
        attended,
        w_out,
        scratch_shapes=[pltpu.VMEM((ROWS, queries, HEAD), f32)],
    )
    hidden = residual + jnp.sum(exchange(part, "tp").astype(f32), axis=0)
    return (
        hidden.reshape(STEPS, ROWS, local_width),
        new_keys.reshape(STEPS, ROWS, HEAD),
        new_values.reshape(STEPS, ROWS, HEAD),
        state,
        history.transpose(1, 0, 2),
    )


def solution(mesh):
    ctx_size, tp_size = mesh.devices.shape
    split = Mesh(
        mesh.devices.reshape(ctx_size // X_SIZE, X_SIZE, tp_size), ("z", "x", "tp")
    )
    return jax.shard_map(
        body,
        mesh=split,
        in_specs=(
            P(None, None, CTX),
            P(CTX),
            P(CTX, "tp"),
            P(CTX, "tp"),
            P(None, "tp"),
            P("tp"),
            P("tp", None),
            P(),
            P(),
            P(),
            P(None, "tp"),
            P("tp"),
            P(None, "tp"),
            P("tp"),
            P("tp", CTX),
            P(CTX),
            P(CTX, "tp"),
            P(CTX, "tp"),
            P(CTX, "tp"),
            P("tp", CTX),
            P(None, CTX, "tp"),
            P(None, CTX, "tp"),
            P(),
            P(None, CTX),
            P(None, None, "tp"),
            P(None, None, "tp"),
        ),
        out_specs=(
            P(None, None, CTX),
            P(None, None, "tp"),
            P(None, None, "tp"),
            P(None, None, "tp"),
            P(None, None, "tp"),
        ),
        check_vma=False,
    )
```

```python
import functools

import jax
import jax.numpy as jnp
from jax import lax
from jax.experimental import pallas as pl
from jax.experimental.pallas import tpu as pltpu
from jax.sharding import Mesh, PartitionSpec as P

DS = 16
DTR = 512
HEAD = 128
BLK = 128
STEPS = 3
ROWS = 8
ALL_ROWS = STEPS * ROWS
LANES = 128
X_SIZE = 4
CTX = ("z", "x")
BLOCKS = 4
FLOPS = 3_000_000_000
NEGATIVE = -1e30
bf16 = jnp.bfloat16
f32 = jnp.float32


def exchange(parts, axis):
    return lax.all_to_all(parts, axis, 0, 0, tiled=True)


def from_partners(part):
    received = {
        flip: lax.ppermute(part, "x", [(i, i ^ flip) for i in range(X_SIZE)])
        for flip in (1, 3, 2)
    }
    return received[1], received[2], received[3]


def call(kernel, outs, *operands, vmem_mib=48, **options):
    return pl.pallas_call(
        kernel,
        out_shape=[jax.ShapeDtypeStruct(shape, dtype) for shape, dtype in outs],
        compiler_params=pltpu.CompilerParams(vmem_limit_bytes=vmem_mib * 1024 * 1024),
        cost_estimate=pl.CostEstimate(flops=FLOPS, bytes_accessed=8 << 20, transcendentals=0),
        **options,
    )(*operands)


def lane_index(rows, lanes=LANES):
    return lax.broadcasted_iota(jnp.int32, (rows, lanes), 1)


def row_index(rows, lanes=LANES):
    return lax.broadcasted_iota(jnp.int32, (rows, lanes), 0)


def rounded(value):
    return value.astype(bf16).astype(f32)


def silu(value):
    return value / (1.0 + jnp.exp(-value))


def project_kernel(
    rows_hbm, gain_hbm, wx_hbm, wz_hbm, out_ref, rows_ref, gain_ref, wx_ref, wz_ref, sems, small_sems
):
    small = [
        pltpu.make_async_copy(rows_hbm, rows_ref, small_sems.at[0]),
        pltpu.make_async_copy(gain_hbm, gain_ref, small_sems.at[1]),
    ]
    for copy in small:
        copy.start()
    cols = wx_ref.shape[1] // BLOCKS
    copies = []
    for i in range(BLOCKS):
        for half, (source, target) in enumerate(((wx_hbm, wx_ref), (wz_hbm, wz_ref))):
            at = slice(i * cols, (i + 1) * cols)
            copies.append(
                pltpu.make_async_copy(source.at[:, at], target.at[:, at], sems.at[half, i])
            )
            copies[-1].start()
    for copy in small:
        copy.wait()
    rows = rows_ref[...].astype(f32)
    scaled = (rows * gain_ref[...]).astype(bf16)
    column = jnp.sum(rows * rows, axis=1, keepdims=True)
    eye = row_index(ALL_ROWS) == lane_index(ALL_ROWS)
    squares = jnp.sum(jnp.where(eye, column, 0.0), axis=0, keepdims=True)
    hi = rounded(squares)
    which = row_index(8)
    stats = jnp.where(which == 0, hi, jnp.where(which == 1, squares - hi, 0.0))
    per = cols // LANES
    for i in range(BLOCKS):
        for half, weight_ref in enumerate((wx_ref, wz_ref)):
            copies[2 * i + half].wait()
            part = jnp.dot(
                scaled, weight_ref[:, i * cols : (i + 1) * cols], preferred_element_type=f32
            )
            for k in range(per):
                chunk = part[:, k * LANES : (k + 1) * LANES]
                out_ref[half, i * per + k] = jnp.concatenate([chunk, stats], axis=0).astype(bf16)


def reduce_kernel(width_all, in_ref, out_ref):
    total = in_ref[0].astype(f32)
    for source in range(1, in_ref.shape[0]):
        total = total + in_ref[source].astype(f32)
    squares = total[ALL_ROWS : ALL_ROWS + 1] + total[ALL_ROWS + 1 : ALL_ROWS + 2]
    eye = row_index(ALL_ROWS) == lane_index(ALL_ROWS)
    column = jnp.sum(jnp.where(eye, squares, 0.0), axis=1, keepdims=True)
    mine = (total[:ALL_ROWS] * lax.rsqrt(column / width_all + 1e-06)).astype(bf16)
    for target in range(out_ref.shape[0]):
        out_ref[target] = mine


def conv_kernel(inner_ref, hist_ref, taps_ref, bias_ref, xp_ref, low_ref, mixed_ref, hist_out_ref, mixed16):
    for k in range(mixed_ref.shape[1] // LANES):
        cols = slice(k * LANES, (k + 1) * LANES)
        fresh = inner_ref[k].astype(f32)
        window = [hist_ref[t, :, cols] for t in range(STEPS)]
        window += [fresh[s * ROWS : (s + 1) * ROWS] for s in range(STEPS)]
        taps = taps_ref[:, cols]
        bias = bias_ref[:, cols]
        mixed = []
        for s in range(STEPS):
            total = window[s] * taps[0:1]
            for t in range(1, STEPS + 1):
                total = total + window[s + t] * taps[t : t + 1]
            mixed.append(silu(total + bias))
            hist_out_ref[s, :, cols] = window[STEPS + s]
        mixed = jnp.concatenate(mixed, axis=0)
        mixed_ref[:, cols] = mixed
        mixed16[:, cols] = mixed.astype(bf16)
    low = lax.dot_general(
        mixed16[...], xp_ref[...], (((1,), (1,)), ((), ())), preferred_element_type=f32
    ).astype(bf16)
    for target in range(low_ref.shape[0]):
        low_ref[target] = low


def scan_kernel(
    low_ref, dt_gain_ref, bc_gain_ref, dt_bias_ref, a_ref, skip_ref, mixed_ref, gate_ref,
    dtp_hbm, state_hbm, op_hbm, state_out_hbm, part_ref,
    dtp_ref, state_ref, op_ref, b_wide, c_wide, y_rows, sems,
):
    channels = mixed_ref.shape[1]
    width = channels // BLOCKS
    copies, leaving = [], []
    for i in range(BLOCKS):
        at = pl.ds(i * width, width)
        copies.append(
            (
                pltpu.make_async_copy(dtp_hbm.at[:, at], dtp_ref.at[:, at], sems.at[0, i]),
                pltpu.make_async_copy(
                    state_hbm.at[:, :, at], state_ref.at[:, :, at], sems.at[1, i]
                ),
                pltpu.make_async_copy(op_hbm.at[at, :], op_ref.at[at, :], sems.at[2, i]),
            )
        )
        leaving.append(
            pltpu.make_async_copy(
                state_ref.at[:, :, at], state_out_hbm.at[:, :, at], sems.at[3, i]
            )
        )
        for copy in copies[-1]:
            copy.start()

    low = low_ref[0].astype(f32)
    for source in range(1, low_ref.shape[0]):
        low = low + low_ref[source].astype(f32)
    raw = low[:, :DTR]
    mean_sq = jnp.sum(raw * raw, axis=1, keepdims=True) / DTR
    dt_low = (raw * lax.rsqrt(mean_sq + 1e-06) * dt_gain_ref[...]).astype(bf16)
    raw = low[:, DTR:]
    is_b = lane_index(ALL_ROWS, 2 * DS) < DS
    squares = raw * raw
    mean_b = jnp.sum(jnp.where(is_b, squares, 0.0), axis=1, keepdims=True) / DS
    mean_c = jnp.sum(jnp.where(is_b, 0.0, squares), axis=1, keepdims=True) / DS
    scale = jnp.where(is_b, lax.rsqrt(mean_b + 1e-06), lax.rsqrt(mean_c + 1e-06))
    normed = raw * scale * bc_gain_ref[...]
    eye_b = lane_index(DS, 2 * DS) == row_index(DS, 2 * DS)
    eye_c = lane_index(DS, 2 * DS) == row_index(DS, 2 * DS) + DS
    for r in range(ALL_ROWS):
        row = normed[r : r + 1]
        for eye, wide in ((eye_b, b_wide), (eye_c, c_wide)):
            column = jnp.sum(jnp.where(eye, row, 0.0), axis=1, keepdims=True)
            wide[r] = jnp.broadcast_to(column, (DS, LANES))

    total = None
    for i in range(BLOCKS):
        block = slice(i * width, (i + 1) * width)
        copies[i][0].wait()
        raw = jnp.dot(dt_low, dtp_ref[:, block], preferred_element_type=f32)
        raw = raw + dt_bias_ref[:, block]
        steps = jnp.maximum(raw, 0.0) + jnp.log1p(jnp.exp(-jnp.abs(raw)))
        mixed = mixed_ref[:, block]
        drive = steps * mixed
        copies[i][1].wait()
        for k in range(width // LANES):
            part = slice(k * LANES, (k + 1) * LANES)
            cols = slice(i * width + k * LANES, i * width + (k + 1) * LANES)
            decay = -jnp.exp(a_ref[:, cols])
            for b in range(ROWS):
                state = state_ref[b, :, cols]
                for s in range(STEPS):
                    r = s * ROWS + b
                    state = (
                        jnp.exp(steps[r : r + 1, part] * decay) * state
                        + drive[r : r + 1, part] * b_wide[r]
                    )
                    y_rows[r : r + 1, cols] = jnp.sum(c_wide[r] * state, axis=0, keepdims=True)
                state_ref[b, :, cols] = state
        leaving[i].start()
        gate = jnp.concatenate(
            [gate_ref[(channels + cols.start) // LANES].astype(f32) for cols in lane_blocks(block)], axis=1
        )
        y = ((y_rows[:, block] + skip_ref[:, block] * mixed) * silu(gate)).astype(bf16)
        copies[i][2].wait()
        product = jnp.dot(y, op_ref[block, :], preferred_element_type=f32)
        total = product if total is None else total + product
    part = total.astype(bf16)
    for target in range(part_ref.shape[0]):
        part_ref[target] = part
    for copy in leaving:
        copy.wait()


def lane_blocks(block):
    return [slice(at, at + LANES) for at in range(block.start, block.stop, LANES)]


def qkv_kernel(parts_ref, rows_ref, gain_ref, wq_ref, wk_ref, wv_ref, residual_ref, out_ref):
    total = parts_ref[0].astype(f32)
    for source in range(1, parts_ref.shape[0]):
        total = total + parts_ref[source].astype(f32)
    residual = rows_ref[...].astype(f32) + total
    residual_ref[...] = residual
    scaled = (residual * gain_ref[...]).astype(bf16)
    column = jnp.sum(residual * residual, axis=1, keepdims=True)
    at = 0
    for weight_ref in (wq_ref, wk_ref, wv_ref):
        width = weight_ref.shape[1]
        out_ref[:, at : at + width] = jnp.dot(
            scaled, weight_ref[...], preferred_element_type=f32
        ).astype(bf16)
        at += width
    out_ref[:, at:] = pair_columns(column).astype(bf16)


def pair_columns(column):
    hi = rounded(column)
    which = lane_index(ALL_ROWS)
    return jnp.where(which == 0, hi, jnp.where(which == 1, column - hi, 0.0))


def qkv_sum_kernel(own_ref, one_ref, two_ref, three_ref, out_ref):
    total = (own_ref[...].astype(f32) + one_ref[...].astype(f32)) + (
        two_ref[...].astype(f32) + three_ref[...].astype(f32)
    )
    column = jnp.sum(total[:, -LANES:], axis=1, keepdims=True)
    body = total[:, :-LANES].astype(bf16)
    last = pair_columns(column).astype(bf16)
    for target in range(out_ref.shape[0]):
        out_ref[target, :, :-LANES] = body
        out_ref[target, :, -LANES:] = last


def pack_logs(logs):
    which = lane_index(ALL_ROWS)
    logs = jnp.where(which < ROWS, logs, 0.0)
    hi = rounded(logs)
    mid = rounded(logs - hi)
    low = logs - hi - mid
    return hi + pltpu.roll(mid, ROWS, 1) + pltpu.roll(low, 2 * ROWS, 1)


def unpack_logs(packed):
    return (
        packed + pltpu.roll(packed, LANES - ROWS, 1) + pltpu.roll(packed, LANES - 2 * ROWS, 1)
    )


def attention_kernel(
    width_all, first_ref, parts_ref, live_ref, keys_ref, values_ref,
    new_keys_ref, new_values_ref, out_ref, query, fresh_k, fresh_v,
):
    total = parts_ref[0].astype(f32)
    for source in range(1, parts_ref.shape[0]):
        total = total + parts_ref[source].astype(f32)
    column = jnp.sum(total[:, -LANES:], axis=1, keepdims=True)
    total = rounded(total[:, :-LANES] * lax.rsqrt(column / width_all + 1e-06))
    heads = total.shape[1] // HEAD - 2
    keys_now = total[:, heads * HEAD : (heads + 1) * HEAD]
    values_now = total[:, (heads + 1) * HEAD :]
    new_keys_ref[...] = keys_now.astype(bf16)
    new_values_ref[...] = values_now.astype(bf16)
    fresh_k[...] = jnp.zeros_like(fresh_k)
    fresh_v[...] = jnp.zeros_like(fresh_v)
    for s in range(STEPS):
        rows = slice(s * ROWS, (s + 1) * ROWS)
        fresh_k[:, s, :] = keys_now[rows]
        fresh_v[:, s, :] = values_now[rows]
        for g in range(heads):
            query[:, s * heads + g, :] = total[rows, g * HEAD : (g + 1) * HEAD]
    queries = STEPS * heads
    which = lane_index(queries, ROWS)
    fresh_live = (which * heads <= row_index(queries, ROWS)) & (which < STEPS)
    fresh_live = fresh_live & (first_ref[0] == 1)
    score_scale = HEAD**-0.5
    lanes = lane_index(queries)
    logs = jnp.zeros((queries, LANES), f32)
    contract = (((1,), (1,)), ((), ()))
    for b in range(ROWS):
        query_b = query[b].astype(bf16)
        live = jnp.broadcast_to(live_ref[b : b + 1, :], (queries, live_ref.shape[1])) > 0
        scores = lax.dot_general(query_b, keys_ref[b], contract, preferred_element_type=f32)
        scores = jnp.where(live, scores * score_scale, NEGATIVE)
        fresh = lax.dot_general(
            query_b, fresh_k[b].astype(bf16), contract, preferred_element_type=f32
        )
        fresh = jnp.where(fresh_live, fresh * score_scale, NEGATIVE)
        peak = jnp.maximum(
            jnp.max(scores, axis=1, keepdims=True), jnp.max(fresh, axis=1, keepdims=True)
        )
        weights = jnp.where(live, jnp.exp(scores - peak), 0.0)
        fresh_weights = jnp.where(fresh_live, jnp.exp(fresh - peak), 0.0)
        weight_sum = jnp.sum(weights, axis=1, keepdims=True) + jnp.sum(
            fresh_weights, axis=1, keepdims=True
        )
        attended = jnp.dot(weights.astype(bf16), values_ref[b], preferred_element_type=f32)
        attended = attended + jnp.dot(
            fresh_weights.astype(bf16), fresh_v[b].astype(bf16), preferred_element_type=f32
        )
        any_live = weight_sum > 0
        safe = jnp.where(any_live, weight_sum, 1.0)
        out_ref[b] = (attended / safe).astype(bf16)
        log_sum = jnp.where(any_live, peak + jnp.log(safe), NEGATIVE)
        logs = jnp.where(lanes == b, log_sum, logs)
    out_ref[ROWS] = pack_logs(logs).astype(bf16)


def shares_of(refs):
    logs = [unpack_logs(ref[ROWS].astype(f32)) for ref in refs]
    top = functools.reduce(jnp.maximum, logs)
    shares = [jnp.exp(log - top) for log in logs]
    total = functools.reduce(jnp.add, shares)
    return [share / total for share in shares], top + jnp.log(total)


def combined_row(refs, shares, b):
    attended = [shares[i][:, b : b + 1] * ref[b].astype(f32) for i, ref in enumerate(refs)]
    return functools.reduce(jnp.add, attended)


def combine_x_kernel(own_ref, one_ref, two_ref, three_ref, out_ref):
    refs = (own_ref, one_ref, two_ref, three_ref)
    shares, logs = shares_of(refs)
    packed = pack_logs(logs).astype(bf16)
    for b in range(ROWS):
        attended = combined_row(refs, shares, b).astype(bf16)
        for target in range(out_ref.shape[0]):
            out_ref[target, b] = attended
    for target in range(out_ref.shape[0]):
        out_ref[target, ROWS] = packed


def combine_z_kernel(parts_ref, weight_ref, out_ref, attended):
    refs = [parts_ref.at[source] for source in range(parts_ref.shape[0])]
    shares, _ = shares_of(refs)
    for b in range(ROWS):
        attended[b] = combined_row(refs, shares, b)
    heads = attended.shape[1] // STEPS
    rows = jnp.concatenate(
        [
            jnp.concatenate([attended[:, s * heads + g, :] for g in range(heads)], axis=1)
            for s in range(STEPS)
        ],
        axis=0,
    ).astype(bf16)
    part = jnp.dot(rows, weight_ref[...], preferred_element_type=f32).astype(bf16)
    for target in range(out_ref.shape[0]):
        out_ref[target] = part


def body(
    embeds, norm_mamba, in_x, in_z, conv_w, conv_b, x_proj, dt_norm, b_norm, c_norm, dt_proj,
    dt_bias, a_log, d_skip, out_proj, norm_attn, w_query, key_matrix, value_matrix, w_out,
    cache_k, value_cache, lengths, block_of_slot, conv_state, ssm_state,
):
    ctx_size, z_size, tp_size = (lax.axis_size(axis) for axis in (CTX, "z", "tp"))
    local_width = embeds.shape[2]
    width_all = float(local_width * ctx_size)
    channels = in_x.shape[1]
    slots = cache_k.shape[1]
    heads = w_query.shape[1] // HEAD
    queries = STEPS * heads
    chunk_count = channels // LANES
    rows_in = embeds.reshape(ALL_ROWS, local_width)

    hbm = pl.BlockSpec(memory_space=pltpu.HBM)
    vmem = pl.BlockSpec(memory_space=pltpu.VMEM)
    (chunks,) = call(
        project_kernel,
        [((2, chunk_count, 32, LANES), bf16)],
        rows_in,
        norm_mamba.reshape(1, -1),
        in_x,
        in_z,
        vmem_mib=62,
        in_specs=[hbm] * 4,
        scratch_shapes=[
            pltpu.VMEM((ALL_ROWS, local_width), bf16),
            pltpu.VMEM((1, local_width), f32),
            pltpu.VMEM(in_x.shape, bf16),
            pltpu.VMEM(in_z.shape, bf16),
            pltpu.SemaphoreType.DMA((2, BLOCKS)),
            pltpu.SemaphoreType.DMA((2,)),
        ],
    )
    received = exchange(chunks.reshape(2 * chunk_count, 32, LANES), CTX)
    (mine,) = call(
        functools.partial(reduce_kernel, width_all),
        [((ctx_size, ALL_ROWS, LANES), bf16)],
        received,
    )
    inner = exchange(mine, CTX)

    low, mixed, history = call(
        conv_kernel,
        [
            ((tp_size, ALL_ROWS, DTR + 2 * DS), bf16),
            ((ALL_ROWS, channels), f32),
            ((STEPS, ROWS, channels), f32),
        ],
        inner,
        conv_state.transpose(1, 0, 2),
        conv_w,
        conv_b.reshape(1, -1),
        x_proj.T,
        scratch_shapes=[pltpu.VMEM((ALL_ROWS, channels), bf16)],
    )
    low = exchange(low, "tp")
    state, part = call(
        scan_kernel,
        [(ssm_state.shape, f32), ((tp_size, ALL_ROWS, local_width), bf16)],
        low,
        dt_norm.reshape(1, -1),
        jnp.concatenate([b_norm, c_norm]).reshape(1, -1),
        dt_bias.reshape(1, -1),
        a_log,
        d_skip.reshape(1, -1),
        mixed,
        inner,
        dt_proj,
        ssm_state,
        out_proj,
        vmem_mib=53,
        in_specs=[vmem] * 8 + [hbm] * 3,
        out_specs=[hbm, vmem],
        scratch_shapes=[
            pltpu.VMEM(dt_proj.shape, bf16),
            pltpu.VMEM(ssm_state.shape, f32),
            pltpu.VMEM(out_proj.shape, bf16),
            pltpu.VMEM((ALL_ROWS, DS, LANES), f32),
            pltpu.VMEM((ALL_ROWS, DS, LANES), f32),
            pltpu.VMEM((ALL_ROWS, channels), f32),
            pltpu.SemaphoreType.DMA((4, BLOCKS)),
        ],
    )
    part = exchange(part, "tp")

    packed_width = (heads + 3) * HEAD
    residual, projected = call(
        qkv_kernel,
        [((ALL_ROWS, local_width), f32), ((ALL_ROWS, packed_width), bf16)],
        part,
        rows_in,
        norm_attn.reshape(1, -1),
        w_query,
        key_matrix,
        value_matrix,
    )
    (projected,) = call(
        qkv_sum_kernel,
        [((z_size, ALL_ROWS, packed_width), bf16)],
        projected,
        *from_partners(projected),
    )
    projected = exchange(projected, "z")

    offsets = jnp.arange(BLK, dtype=jnp.int32)
    positions = (block_of_slot[:, :, None] * BLK + offsets[None, None, :]).reshape(ROWS, slots)
    live = (positions < lengths[:, None]).astype(f32)
    first = (lax.axis_index(CTX) == 0).astype(jnp.int32).reshape(1)
    new_keys, new_values, attended = call(
        functools.partial(attention_kernel, width_all),
        [
            ((ALL_ROWS, HEAD), bf16),
            ((ALL_ROWS, HEAD), bf16),
            ((ROWS + 1, queries, HEAD), bf16),
        ],
        first,
        projected,
        live,
        cache_k,
        value_cache,
        in_specs=[pl.BlockSpec(memory_space=pltpu.SMEM)] + [vmem] * 4,
        scratch_shapes=[
            pltpu.VMEM((ROWS, queries, HEAD), f32),
            pltpu.VMEM((ROWS, 8, HEAD), f32),
            pltpu.VMEM((ROWS, 8, HEAD), f32),
        ],
    )
    (attended,) = call(
        combine_x_kernel,
        [((z_size,) + attended.shape, bf16)],
        attended,
        *from_partners(attended),
    )
    attended = exchange(attended, "z")
    (part,) = call(
        combine_z_kernel,
        [((tp_size, ALL_ROWS, local_width), bf16)],
        attended,
        w_out,
        scratch_shapes=[pltpu.VMEM((ROWS, queries, HEAD), f32)],
    )
    hidden = residual + jnp.sum(exchange(part, "tp").astype(f32), axis=0)
    return (
        hidden.reshape(STEPS, ROWS, local_width),
        new_keys.reshape(STEPS, ROWS, HEAD),
        new_values.reshape(STEPS, ROWS, HEAD),
        state,
        history.transpose(1, 0, 2),
    )


def solution(mesh):
    ctx_size, tp_size = mesh.devices.shape
    split = Mesh(
        mesh.devices.reshape(ctx_size // X_SIZE, X_SIZE, tp_size), ("z", "x", "tp")
    )
    return jax.shard_map(
        body,
        mesh=split,
        in_specs=(
            P(None, None, CTX),
            P(CTX),
            P(CTX, "tp"),
            P(CTX, "tp"),
            P(None, "tp"),
            P("tp"),
            P("tp", None),
            P(),
            P(),
            P(),
            P(None, "tp"),
            P("tp"),
            P(None, "tp"),
            P("tp"),
            P("tp", CTX),
            P(CTX),
            P(CTX, "tp"),
            P(CTX, "tp"),
            P(CTX, "tp"),
            P("tp", CTX),
            P(None, CTX, "tp"),
            P(None, CTX, "tp"),
            P(),
            P(None, CTX),
            P(None, None, "tp"),
            P(None, None, "tp"),
        ),
        out_specs=(
            P(None, None, CTX),
            P(None, None, "tp"),
            P(None, None, "tp"),
            P(None, None, "tp"),
            P(None, None, "tp"),
        ),
        check_vma=False,
    )
```

```python
import functools

import jax
import jax.numpy as jnp
from jax import lax
from jax.experimental import pallas as pl
from jax.experimental.pallas import tpu as pltpu
from jax.sharding import Mesh, PartitionSpec as P

DS = 16
DTR = 512
HEAD = 128
BLK = 128
STEPS = 3
ROWS = 8
ALL_ROWS = STEPS * ROWS
LANES = 128
X_SIZE = 4
CTX = ("z", "x")
FLOPS = 3_000_000_000
GROUPS = 4
NEGATIVE = -1e30
bf16 = jnp.bfloat16
f32 = jnp.float32


def exchange(parts, axis):
    return lax.all_to_all(parts, axis, 0, 0, tiled=True)


def from_partners(part):
    received = {
        flip: lax.ppermute(part, "x", [(i, i ^ flip) for i in range(X_SIZE)])
        for flip in (1, 3, 2)
    }
    return received[1], received[2], received[3]


def call(kernel, outs, *operands, vmem_mib=48, **options):
    return pl.pallas_call(
        kernel,
        out_shape=[jax.ShapeDtypeStruct(shape, dtype) for shape, dtype in outs],
        compiler_params=pltpu.CompilerParams(vmem_limit_bytes=vmem_mib * 1024 * 1024),
        cost_estimate=pl.CostEstimate(flops=FLOPS, bytes_accessed=8 << 20, transcendentals=0),
        **options,
    )(*operands)


def lane_index(rows, lanes=LANES):
    return lax.broadcasted_iota(jnp.int32, (rows, lanes), 1)


def row_index(rows, lanes=LANES):
    return lax.broadcasted_iota(jnp.int32, (rows, lanes), 0)


def rounded(value):
    return value.astype(bf16).astype(f32)


def silu(value):
    return value / (1.0 + jnp.exp(-value))


def project_kernel(
    rows_hbm, gain_hbm, wx_hbm, wz_hbm, out_ref, rows_ref, gain_ref, wx_ref, wz_ref, sems, small_sems
):
    small = [
        pltpu.make_async_copy(rows_hbm, rows_ref, small_sems.at[0]),
        pltpu.make_async_copy(gain_hbm, gain_ref, small_sems.at[1]),
    ]
    for copy in small:
        copy.start()
    copies = []
    for half, (source, target) in enumerate(((wx_hbm, wx_ref), (wz_hbm, wz_ref))):
        copies.append(pltpu.make_async_copy(source, target, sems.at[half]))
        copies[-1].start()
    for copy in small:
        copy.wait()
    rows = rows_ref[...].astype(f32)
    scaled = (rows * gain_ref[...]).astype(bf16)
    column = jnp.sum(rows * rows, axis=1, keepdims=True)
    eye = row_index(ALL_ROWS) == lane_index(ALL_ROWS)
    squares = jnp.sum(jnp.where(eye, column, 0.0), axis=0, keepdims=True)
    hi = rounded(squares)
    which = row_index(8)
    stats = jnp.where(which == 0, hi, jnp.where(which == 1, squares - hi, 0.0))
    for half, weight_ref in enumerate((wx_ref, wz_ref)):
        copies[half].wait()
        part = jnp.dot(scaled, weight_ref[...], preferred_element_type=f32)
        for k in range(out_ref.shape[1]):
            chunk = part[:, k * LANES : (k + 1) * LANES]
            out_ref[half, k] = jnp.concatenate([chunk, stats], axis=0).astype(bf16)


def reduce_kernel(width_all, in_ref, out_ref):
    total = in_ref[0].astype(f32)
    for source in range(1, in_ref.shape[0]):
        total = total + in_ref[source].astype(f32)
    squares = total[ALL_ROWS : ALL_ROWS + 1] + total[ALL_ROWS + 1 : ALL_ROWS + 2]
    eye = row_index(ALL_ROWS) == lane_index(ALL_ROWS)
    column = jnp.sum(jnp.where(eye, squares, 0.0), axis=1, keepdims=True)
    mine = (total[:ALL_ROWS] * lax.rsqrt(column / width_all + 1e-06)).astype(bf16)
    for target in range(out_ref.shape[0]):
        out_ref[target] = mine


def conv_kernel(inner_ref, hist_ref, taps_ref, bias_ref, xp_ref, low_ref, mixed_ref, hist_out_ref, mixed16):
    for k in range(mixed_ref.shape[1] // LANES):
        cols = slice(k * LANES, (k + 1) * LANES)
        fresh = inner_ref[k].astype(f32)
        window = [hist_ref[t, :, cols] for t in range(STEPS)]
        window += [fresh[s * ROWS : (s + 1) * ROWS] for s in range(STEPS)]
        taps = taps_ref[:, cols]
        bias = bias_ref[:, cols]
        mixed = []
        for s in range(STEPS):
            total = window[s] * taps[0:1]
            for t in range(1, STEPS + 1):
                total = total + window[s + t] * taps[t : t + 1]
            mixed.append(silu(total + bias))
            hist_out_ref[s, :, cols] = window[STEPS + s]
        mixed = jnp.concatenate(mixed, axis=0)
        mixed_ref[:, cols] = mixed
        mixed16[:, cols] = mixed.astype(bf16)
    low = lax.dot_general(
        mixed16[...], xp_ref[...], (((1,), (1,)), ((), ())), preferred_element_type=f32
    ).astype(bf16)
    for target in range(low_ref.shape[0]):
        low_ref[target] = low


def scan_kernel(
    low_ref, dt_gain_ref, b_gain_ref, c_gain_ref, dt_bias_ref, a_ref, skip_ref, mixed_ref, gate_ref,
    state_hbm, dtp_hbm, op_hbm, state_out_hbm, part_ref,
    dtp_ref, op_ref, state_ref, b_wide, c_wide, decay_wide, sems, state_sems,
):
    tiles = state_ref.shape[0]
    group = tiles // GROUPS
    dtp_copy = pltpu.make_async_copy(dtp_hbm, dtp_ref, sems.at[0])
    op_copy = pltpu.make_async_copy(op_hbm, op_ref, sems.at[1])
    dtp_copy.start()
    entering, leaving = [], []
    for i in range(GROUPS):
        at = pl.ds(i * group, group)
        entering.append(
            pltpu.make_async_copy(state_hbm.at[at], state_ref.at[at], state_sems.at[0, i])
        )
        entering[i].start()
        leaving.append(
            pltpu.make_async_copy(state_ref.at[at], state_out_hbm.at[at], state_sems.at[1, i])
        )
    op_copy.start()
    low = low_ref[0].astype(f32)
    for source in range(1, low_ref.shape[0]):
        low = low + low_ref[source].astype(f32)
    raw = low[:, :DTR]
    mean_sq = jnp.sum(raw * raw, axis=1, keepdims=True) / DTR
    dt_low = (raw * lax.rsqrt(mean_sq + 1e-06) * dt_gain_ref[...]).astype(bf16)
    for wide, gain_ref, at in ((b_wide, b_gain_ref, DTR), (c_wide, c_gain_ref, DTR + DS)):
        raw = low[:, at : at + DS]
        mean_sq = jnp.sum(raw * raw, axis=1, keepdims=True) / DS
        normed = raw * lax.rsqrt(mean_sq + 1e-06) * gain_ref[...]
        for n in range(DS):
            wide[n] = jnp.broadcast_to(normed[:, n : n + 1], (ALL_ROWS, LANES))
    for tile in range(tiles):
        decay = -jnp.exp(a_ref[:, tile * LANES : (tile + 1) * LANES])
        for n in range(DS):
            decay_wide[tile, n] = jnp.broadcast_to(decay[n : n + 1], (ROWS, LANES))
    dtp_copy.wait()
    raw = jnp.dot(dt_low, dtp_ref[...], preferred_element_type=f32) + dt_bias_ref[...]
    steps = jnp.maximum(raw, 0.0) + jnp.log1p(jnp.exp(-jnp.abs(raw)))
    mixed = mixed_ref[...]
    drive = steps * mixed
    scanned = []
    for tile in range(tiles):
        cols = slice(tile * LANES, (tile + 1) * LANES)
        if tile % group == 0:
            entering[tile // group].wait()
        y = [jnp.zeros((ROWS, LANES), f32) for _ in range(STEPS)]
        for n in range(DS):
            state = state_ref[tile, n]
            decay = decay_wide[tile, n]
            for s in range(STEPS):
                rows = slice(s * ROWS, (s + 1) * ROWS)
                state = (
                    jnp.exp(steps[rows, cols] * decay) * state + drive[rows, cols] * b_wide[n, rows]
                )
                y[s] = y[s] + c_wide[n, rows] * state
            state_ref[tile, n] = state
        if tile % group == group - 1:
            leaving[tile // group].start()
        y = jnp.concatenate(y, axis=0) + skip_ref[:, cols] * mixed[:, cols]
        scanned.append((y * silu(gate_ref[tiles + tile].astype(f32))).astype(bf16))
    op_copy.wait()
    total = jnp.dot(jnp.concatenate(scanned, axis=1), op_ref[...], preferred_element_type=f32)
    part = total.astype(bf16)
    for target in range(part_ref.shape[0]):
        part_ref[target] = part
    for copy in leaving:
        copy.wait()


def qkv_kernel(parts_ref, rows_ref, gain_ref, wq_ref, wk_ref, wv_ref, residual_ref, out_ref):
    total = parts_ref[0].astype(f32)
    for source in range(1, parts_ref.shape[0]):
        total = total + parts_ref[source].astype(f32)
    residual = rows_ref[...].astype(f32) + total
    residual_ref[...] = residual
    scaled = (residual * gain_ref[...]).astype(bf16)
    column = jnp.sum(residual * residual, axis=1, keepdims=True)
    at = 0
    for weight_ref in (wq_ref, wk_ref, wv_ref):
        width = weight_ref.shape[1]
        out_ref[:, at : at + width] = jnp.dot(
            scaled, weight_ref[...], preferred_element_type=f32
        ).astype(bf16)
        at += width
    out_ref[:, at:] = pair_columns(column).astype(bf16)


def pair_columns(column):
    hi = rounded(column)
    which = lane_index(ALL_ROWS)
    return jnp.where(which == 0, hi, jnp.where(which == 1, column - hi, 0.0))


def qkv_sum_kernel(own_ref, one_ref, two_ref, three_ref, out_ref):
    total = (own_ref[...].astype(f32) + one_ref[...].astype(f32)) + (
        two_ref[...].astype(f32) + three_ref[...].astype(f32)
    )
    column = jnp.sum(total[:, -LANES:], axis=1, keepdims=True)
    body = total[:, :-LANES].astype(bf16)
    last = pair_columns(column).astype(bf16)
    for target in range(out_ref.shape[0]):
        out_ref[target, :, :-LANES] = body
        out_ref[target, :, -LANES:] = last


def pack_logs(logs):
    which = lane_index(ALL_ROWS)
    logs = jnp.where(which < ROWS, logs, 0.0)
    hi = rounded(logs)
    mid = rounded(logs - hi)
    low = logs - hi - mid
    return hi + pltpu.roll(mid, ROWS, 1) + pltpu.roll(low, 2 * ROWS, 1)


def unpack_logs(packed):
    return (
        packed + pltpu.roll(packed, LANES - ROWS, 1) + pltpu.roll(packed, LANES - 2 * ROWS, 1)
    )


def attention_kernel(
    width_all, first_ref, lengths_ref, blocks_ref, parts_ref, keys_ref, values_ref,
    new_keys_ref, new_values_ref, out_ref, query, fresh_k, fresh_v,
):
    total = parts_ref[0].astype(f32)
    for source in range(1, parts_ref.shape[0]):
        total = total + parts_ref[source].astype(f32)
    column = jnp.sum(total[:, -LANES:], axis=1, keepdims=True)
    total = rounded(total[:, :-LANES] * lax.rsqrt(column / width_all + 1e-06))
    heads = total.shape[1] // HEAD - 2
    queries = STEPS * heads
    keys_now = total[:, heads * HEAD : (heads + 1) * HEAD]
    values_now = total[:, (heads + 1) * HEAD :]
    new_keys_ref[...] = keys_now.astype(bf16)
    new_values_ref[...] = values_now.astype(bf16)
    fresh_k[...] = jnp.zeros_like(fresh_k)
    fresh_v[...] = jnp.zeros_like(fresh_v)
    for s in range(STEPS):
        rows = slice(s * ROWS, (s + 1) * ROWS)
        fresh_k[pl.ds(s, ROWS, stride=8), :] = keys_now[rows]
        fresh_v[pl.ds(s, ROWS, stride=8), :] = values_now[rows]
        for g in range(heads):
            query[pl.ds(s * heads + g, ROWS, stride=queries), :] = total[
                rows, g * HEAD : (g + 1) * HEAD
            ]
    which = lane_index(queries, 8)
    fresh_live = (which * heads <= row_index(queries, 8)) & (which < STEPS)
    fresh_live = fresh_live & (first_ref[0] == 1)
    score_scale = HEAD**-0.5
    lanes = lane_index(queries)
    contract = (((1,), (1,)), ((), ()))
    every = range(ROWS)
    scores, fresh, live = [], [], []
    for b in every:
        query_b = query[b * queries : (b + 1) * queries, :].astype(bf16)
        scores.append(
            lax.dot_general(query_b, keys_ref[b], contract, preferred_element_type=f32)
        )
        fresh.append(
            lax.dot_general(
                query_b,
                fresh_k[b * 8 : (b + 1) * 8, :].astype(bf16),
                contract,
                preferred_element_type=f32,
            )
        )
        live.append(
            jnp.concatenate(
                [
                    lanes < lengths_ref[b] - blocks_ref[k, b] * BLK
                    for k in range(keys_ref.shape[1] // BLK)
                ],
                axis=1,
            )
        )
    scores = [jnp.where(live[b], scores[b] * score_scale, NEGATIVE) for b in every]
    fresh = [jnp.where(fresh_live, fresh[b] * score_scale, NEGATIVE) for b in every]
    peaks = [
        jnp.maximum(
            jnp.max(scores[b], axis=1, keepdims=True), jnp.max(fresh[b], axis=1, keepdims=True)
        )
        for b in every
    ]
    weights = [jnp.where(live[b], jnp.exp(scores[b] - peaks[b]), 0.0) for b in every]
    fresh = [jnp.where(fresh_live, jnp.exp(fresh[b] - peaks[b]), 0.0) for b in every]
    attended = [
        jnp.dot(weights[b].astype(bf16), values_ref[b], preferred_element_type=f32)
        + jnp.dot(
            fresh[b].astype(bf16),
            fresh_v[b * 8 : (b + 1) * 8, :].astype(bf16),
            preferred_element_type=f32,
        )
        for b in every
    ]
    sums = [
        jnp.sum(weights[b], axis=1, keepdims=True) + jnp.sum(fresh[b], axis=1, keepdims=True)
        for b in every
    ]
    logs = jnp.zeros((queries, LANES), f32)
    for b in every:
        any_live = sums[b] > 0
        safe = jnp.where(any_live, sums[b], 1.0)
        out_ref[b] = (attended[b] / safe).astype(bf16)
        log_sum = jnp.where(any_live, peaks[b] + jnp.log(safe), NEGATIVE)
        logs = jnp.where(lanes == b, log_sum, logs)
    out_ref[ROWS] = pack_logs(logs).astype(bf16)


def shares_of(refs):
    logs = [unpack_logs(ref[ROWS].astype(f32)) for ref in refs]
    top = functools.reduce(jnp.maximum, logs)
    shares = [jnp.exp(log - top) for log in logs]
    total = functools.reduce(jnp.add, shares)
    return [share / total for share in shares], top + jnp.log(total)


def combined_row(refs, shares, b):
    attended = [shares[i][:, b : b + 1] * ref[b].astype(f32) for i, ref in enumerate(refs)]
    return functools.reduce(jnp.add, attended)


def combine_x_kernel(own_ref, one_ref, two_ref, three_ref, out_ref):
    refs = (own_ref, one_ref, two_ref, three_ref)
    shares, logs = shares_of(refs)
    packed = pack_logs(logs).astype(bf16)
    for b in range(ROWS):
        attended = combined_row(refs, shares, b).astype(bf16)
        for target in range(out_ref.shape[0]):
            out_ref[target, b] = attended
    for target in range(out_ref.shape[0]):
        out_ref[target, ROWS] = packed


def combine_z_kernel(parts_ref, weight_ref, out_ref, attended):
    refs = [parts_ref.at[source] for source in range(parts_ref.shape[0])]
    shares, _ = shares_of(refs)
    for b in range(ROWS):
        queries = shares[0].shape[0]
        attended[b * queries : (b + 1) * queries, :] = combined_row(refs, shares, b)
    heads = queries // STEPS
    rows = jnp.concatenate(
        [
            jnp.concatenate(
                [
                    attended[pl.ds(s * heads + g, ROWS, stride=queries), :]
                    for g in range(heads)
                ],
                axis=1,
            )
            for s in range(STEPS)
        ],
        axis=0,
    ).astype(bf16)
    part = jnp.dot(rows, weight_ref[...], preferred_element_type=f32).astype(bf16)
    for target in range(out_ref.shape[0]):
        out_ref[target] = part


def body(
    embeds, norm_mamba, in_x, in_z, conv_w, conv_b, x_proj, dt_norm, b_norm, c_norm, dt_proj,
    dt_bias, a_log, d_skip, out_proj, norm_attn, w_query, key_matrix, value_matrix, w_out,
    cache_k, value_cache, lengths, block_of_slot, conv_state, ssm_state,
):
    ctx_size, z_size, tp_size = (lax.axis_size(axis) for axis in (CTX, "z", "tp"))
    local_width = embeds.shape[2]
    width_all = float(local_width * ctx_size)
    channels = in_x.shape[1]
    heads = w_query.shape[1] // HEAD
    queries = STEPS * heads
    chunk_count = channels // LANES
    rows_in = embeds.reshape(ALL_ROWS, local_width)

    hbm = pl.BlockSpec(memory_space=pltpu.HBM)
    vmem = pl.BlockSpec(memory_space=pltpu.VMEM)
    (chunks,) = call(
        project_kernel,
        [((2, chunk_count, 32, LANES), bf16)],
        rows_in,
        norm_mamba.reshape(1, -1),
        in_x,
        in_z,
        vmem_mib=62,
        in_specs=[hbm] * 4,
        scratch_shapes=[
            pltpu.VMEM((ALL_ROWS, local_width), bf16),
            pltpu.VMEM((1, local_width), f32),
            pltpu.VMEM(in_x.shape, bf16),
            pltpu.VMEM(in_z.shape, bf16),
            pltpu.SemaphoreType.DMA((2,)),
            pltpu.SemaphoreType.DMA((2,)),
        ],
    )
    received = exchange(chunks.reshape(2 * chunk_count, 32, LANES), CTX)
    (mine,) = call(
        functools.partial(reduce_kernel, width_all),
        [((ctx_size, ALL_ROWS, LANES), bf16)],
        received,
    )
    inner = exchange(mine, CTX)

    low, mixed, history = call(
        conv_kernel,
        [
            ((tp_size, ALL_ROWS, DTR + 2 * DS), bf16),
            ((ALL_ROWS, channels), f32),
            ((STEPS, ROWS, channels), f32),
        ],
        inner,
        conv_state.transpose(1, 0, 2),
        conv_w,
        conv_b.reshape(1, -1),
        x_proj.T,
        scratch_shapes=[pltpu.VMEM((ALL_ROWS, channels), bf16)],
    )
    low = exchange(low, "tp")
    tiled = (chunk_count, DS, ROWS, LANES)
    state = ssm_state.reshape(ROWS, DS, chunk_count, LANES).transpose(2, 1, 0, 3)
    state, part = call(
        scan_kernel,
        [(tiled, f32), ((tp_size, ALL_ROWS, local_width), bf16)],
        low,
        dt_norm.reshape(1, -1),
        b_norm.reshape(1, -1),
        c_norm.reshape(1, -1),
        dt_bias.reshape(1, -1),
        a_log,
        d_skip.reshape(1, -1),
        mixed,
        inner,
        state,
        dt_proj,
        out_proj,
        vmem_mib=53,
        in_specs=[vmem] * 9 + [hbm] * 3,
        out_specs=[hbm, vmem],
        scratch_shapes=[
            pltpu.VMEM(dt_proj.shape, bf16),
            pltpu.VMEM(out_proj.shape, bf16),
            pltpu.VMEM(tiled, f32),
            pltpu.VMEM((DS, ALL_ROWS, LANES), f32),
            pltpu.VMEM((DS, ALL_ROWS, LANES), f32),
            pltpu.VMEM(tiled, f32),
            pltpu.SemaphoreType.DMA((2,)),
            pltpu.SemaphoreType.DMA((2, GROUPS)),
        ],
    )
    state = state.transpose(2, 1, 0, 3).reshape(ssm_state.shape)
    part = exchange(part, "tp")

    packed_width = (heads + 3) * HEAD
    residual, projected = call(
        qkv_kernel,
        [((ALL_ROWS, local_width), f32), ((ALL_ROWS, packed_width), bf16)],
        part,
        rows_in,
        norm_attn.reshape(1, -1),
        w_query,
        key_matrix,
        value_matrix,
    )
    (projected,) = call(
        qkv_sum_kernel,
        [((z_size, ALL_ROWS, packed_width), bf16)],
        projected,
        *from_partners(projected),
    )
    projected, state = lax.optimization_barrier((exchange(projected, "z"), state))

    first = (lax.axis_index(CTX) == 0).astype(jnp.int32).reshape(1)
    new_keys, new_values, attended = call(
        functools.partial(attention_kernel, width_all),
        [
            ((ALL_ROWS, HEAD), bf16),
            ((ALL_ROWS, HEAD), bf16),
            ((ROWS + 1, queries, HEAD), bf16),
        ],
        first,
        lengths,
        block_of_slot.T,
        projected,
        cache_k,
        value_cache,
        in_specs=[pl.BlockSpec(memory_space=pltpu.SMEM)] * 3 + [vmem] * 3,
        scratch_shapes=[
            pltpu.VMEM((ROWS * queries, HEAD), f32),
            pltpu.VMEM((ROWS * 8, HEAD), f32),
            pltpu.VMEM((ROWS * 8, HEAD), f32),
        ],
    )
    (attended,) = call(
        combine_x_kernel,
        [((z_size,) + attended.shape, bf16)],
        attended,
        *from_partners(attended),
    )
    attended = exchange(attended, "z")
    (part,) = call(
        combine_z_kernel,
        [((tp_size, ALL_ROWS, local_width), bf16)],
        attended,
        w_out,
        scratch_shapes=[pltpu.VMEM((ROWS * queries, HEAD), f32)],
    )
    hidden = residual + jnp.sum(exchange(part, "tp").astype(f32), axis=0)
    return (
        hidden.reshape(STEPS, ROWS, local_width),
        new_keys.reshape(STEPS, ROWS, HEAD),
        new_values.reshape(STEPS, ROWS, HEAD),
        state,
        history.transpose(1, 0, 2),
    )


def solution(mesh):
    ctx_size, tp_size = mesh.devices.shape
    split = Mesh(
        mesh.devices.reshape(ctx_size // X_SIZE, X_SIZE, tp_size), ("z", "x", "tp")
    )
    return jax.shard_map(
        body,
        mesh=split,
        in_specs=(
            P(None, None, CTX),
            P(CTX),
            P(CTX, "tp"),
            P(CTX, "tp"),
            P(None, "tp"),
            P("tp"),
            P("tp", None),
            P(),
            P(),
            P(),
            P(None, "tp"),
            P("tp"),
            P(None, "tp"),
            P("tp"),
            P("tp", CTX),
            P(CTX),
            P(CTX, "tp"),
            P(CTX, "tp"),
            P(CTX, "tp"),
            P("tp", CTX),
            P(None, CTX, "tp"),
            P(None, CTX, "tp"),
            P(),
            P(None, CTX),
            P(None, None, "tp"),
            P(None, None, "tp"),
        ),
        out_specs=(
            P(None, None, CTX),
            P(None, None, "tp"),
            P(None, None, "tp"),
            P(None, None, "tp"),
            P(None, None, "tp"),
        ),
        check_vma=False,
    )
```

```python
import functools

import jax
import jax.numpy as jnp
from jax import lax
from jax.experimental import pallas as pl
from jax.experimental.pallas import tpu as pltpu
from jax.sharding import Mesh, PartitionSpec as P

DS = 16
DTR = 512
HEAD = 128
BLK = 128
STEPS = 3
ROWS = 8
ALL_ROWS = STEPS * ROWS
LANES = 128
X_SIZE = 4
CTX = ("za", "zb", "x")
TP = ("y", "core")
FLOPS = 3_000_000_000
GROUPS = 4
NEGATIVE = -1e30
bf16 = jnp.bfloat16
f32 = jnp.float32


def exchange(parts, axis):
    return lax.all_to_all(parts, axis, 0, 0, tiled=True)


def from_partners(part, axis="x"):
    received = {
        flip: lax.ppermute(part, axis, [(i, i ^ flip) for i in range(4)]) for flip in (1, 3, 2)
    }
    return received[1], received[2], received[3]


def from_other(part, axis):
    return lax.ppermute(part, axis, [(0, 1), (1, 0)])


def over_cores(part):
    return part + from_other(part, "core")


def call(kernel, outs, *operands, vmem_mib=48, **options):
    return pl.pallas_call(
        kernel,
        out_shape=[jax.ShapeDtypeStruct(shape, dtype) for shape, dtype in outs],
        compiler_params=pltpu.CompilerParams(vmem_limit_bytes=vmem_mib * 1024 * 1024),
        cost_estimate=pl.CostEstimate(flops=FLOPS, bytes_accessed=8 << 20, transcendentals=0),
        **options,
    )(*operands)


def lane_index(rows, lanes=LANES):
    return lax.broadcasted_iota(jnp.int32, (rows, lanes), 1)


def row_index(rows, lanes=LANES):
    return lax.broadcasted_iota(jnp.int32, (rows, lanes), 0)


def rounded(value):
    return value.astype(bf16).astype(f32)


def silu(value):
    return value / (1.0 + jnp.exp(-value))


def project_kernel(
    rows_hbm, gain_hbm, wx_hbm, wz_hbm, out_ref, rows_ref, gain_ref, wx_ref, wz_ref, sems, small_sems
):
    small = [
        pltpu.make_async_copy(rows_hbm, rows_ref, small_sems.at[0]),
        pltpu.make_async_copy(gain_hbm, gain_ref, small_sems.at[1]),
    ]
    for copy in small:
        copy.start()
    copies = []
    for half, (source, target) in enumerate(((wx_hbm, wx_ref), (wz_hbm, wz_ref))):
        copies.append(pltpu.make_async_copy(source, target, sems.at[half]))
        copies[-1].start()
    for copy in small:
        copy.wait()
    rows = rows_ref[...].astype(f32)
    scaled = (rows * gain_ref[...]).astype(bf16)
    column = jnp.sum(rows * rows, axis=1, keepdims=True)
    eye = row_index(ALL_ROWS) == lane_index(ALL_ROWS)
    squares = jnp.sum(jnp.where(eye, column, 0.0), axis=0, keepdims=True)
    hi = rounded(squares)
    which = row_index(8)
    stats = jnp.where(which == 0, hi, jnp.where(which == 1, squares - hi, 0.0))
    for half, weight_ref in enumerate((wx_ref, wz_ref)):
        copies[half].wait()
        part = jnp.dot(scaled, weight_ref[...], preferred_element_type=f32)
        for k in range(out_ref.shape[1]):
            chunk = part[:, k * LANES : (k + 1) * LANES]
            out_ref[half, k] = jnp.concatenate([chunk, stats], axis=0).astype(bf16)


def reduce_kernel(width_all, in_ref, out_ref):
    total = in_ref[0].astype(f32)
    for source in range(1, in_ref.shape[0]):
        total = total + in_ref[source].astype(f32)
    squares = total[ALL_ROWS : ALL_ROWS + 1] + total[ALL_ROWS + 1 : ALL_ROWS + 2]
    eye = row_index(ALL_ROWS) == lane_index(ALL_ROWS)
    column = jnp.sum(jnp.where(eye, squares, 0.0), axis=1, keepdims=True)
    mine = (total[:ALL_ROWS] * lax.rsqrt(column / width_all + 1e-06)).astype(bf16)
    for target in range(out_ref.shape[0]):
        out_ref[target] = mine


def conv_kernel(inner_ref, hist_ref, taps_ref, bias_ref, xp_ref, low_ref, mixed_ref, hist_out_ref, mixed16):
    for k in range(mixed_ref.shape[1] // LANES):
        cols = slice(k * LANES, (k + 1) * LANES)
        fresh = inner_ref[k].astype(f32)
        window = [hist_ref[t, :, cols] for t in range(STEPS)]
        window += [fresh[s * ROWS : (s + 1) * ROWS] for s in range(STEPS)]
        taps = taps_ref[:, cols]
        bias = bias_ref[:, cols]
        mixed = []
        for s in range(STEPS):
            total = window[s] * taps[0:1]
            for t in range(1, STEPS + 1):
                total = total + window[s + t] * taps[t : t + 1]
            mixed.append(silu(total + bias))
            hist_out_ref[s, :, cols] = window[STEPS + s]
        mixed = jnp.concatenate(mixed, axis=0)
        mixed_ref[:, cols] = mixed
        mixed16[:, cols] = mixed.astype(bf16)
    low = lax.dot_general(
        mixed16[...], xp_ref[...], (((1,), (1,)), ((), ())), preferred_element_type=f32
    ).astype(bf16)
    low_ref[...] = low


def scan_kernel(
    own_ref, one_ref, two_ref, three_ref, dt_gain_ref, b_gain_ref, c_gain_ref, dt_bias_ref, a_ref, skip_ref, mixed_ref, gate_ref,
    state_hbm, dtp_hbm, op_hbm, state_out_hbm, part_ref,
    dtp_ref, op_ref, state_ref, b_wide, c_wide, decay_wide, sems, state_sems,
):
    tiles = state_ref.shape[0]
    group = tiles // GROUPS
    dtp_copy = pltpu.make_async_copy(dtp_hbm, dtp_ref, sems.at[0])
    op_copy = pltpu.make_async_copy(op_hbm, op_ref, sems.at[1])
    dtp_copy.start()
    entering, leaving = [], []
    for i in range(GROUPS):
        at = pl.ds(i * group, group)
        entering.append(
            pltpu.make_async_copy(state_hbm.at[at], state_ref.at[at], state_sems.at[0, i])
        )
        entering[i].start()
        leaving.append(
            pltpu.make_async_copy(state_ref.at[at], state_out_hbm.at[at], state_sems.at[1, i])
        )
    op_copy.start()
    low = sum_refs((own_ref, one_ref, two_ref, three_ref))
    raw = low[:, :DTR]
    mean_sq = jnp.sum(raw * raw, axis=1, keepdims=True) / DTR
    dt_low = (raw * lax.rsqrt(mean_sq + 1e-06) * dt_gain_ref[...]).astype(bf16)
    for wide, gain_ref, at in ((b_wide, b_gain_ref, DTR), (c_wide, c_gain_ref, DTR + DS)):
        raw = low[:, at : at + DS]
        mean_sq = jnp.sum(raw * raw, axis=1, keepdims=True) / DS
        normed = raw * lax.rsqrt(mean_sq + 1e-06) * gain_ref[...]
        for n in range(DS):
            wide[n] = jnp.broadcast_to(normed[:, n : n + 1], (ALL_ROWS, LANES))
    for tile in range(tiles):
        decay = -jnp.exp(a_ref[:, tile * LANES : (tile + 1) * LANES])
        for n in range(DS):
            decay_wide[tile, n] = jnp.broadcast_to(decay[n : n + 1], (ROWS, LANES))
    dtp_copy.wait()
    raw = jnp.dot(dt_low, dtp_ref[...], preferred_element_type=f32) + dt_bias_ref[...]
    steps = jnp.maximum(raw, 0.0) + jnp.log1p(jnp.exp(-jnp.abs(raw)))
    mixed = mixed_ref[...]
    drive = steps * mixed
    scanned = []
    for tile in range(tiles):
        cols = slice(tile * LANES, (tile + 1) * LANES)
        if tile % group == 0:
            entering[tile // group].wait()
        y = [jnp.zeros((ROWS, LANES), f32) for _ in range(STEPS)]
        for n in range(DS):
            state = state_ref[tile, n]
            decay = decay_wide[tile, n]
            for s in range(STEPS):
                rows = slice(s * ROWS, (s + 1) * ROWS)
                state = (
                    jnp.exp(steps[rows, cols] * decay) * state + drive[rows, cols] * b_wide[n, rows]
                )
                y[s] = y[s] + c_wide[n, rows] * state
            state_ref[tile, n] = state
        if tile % group == group - 1:
            leaving[tile // group].start()
        y = jnp.concatenate(y, axis=0) + skip_ref[:, cols] * mixed[:, cols]
        scanned.append((y * silu(gate_ref[tiles + tile].astype(f32))).astype(bf16))
    op_copy.wait()
    total = jnp.dot(jnp.concatenate(scanned, axis=1), op_ref[...], preferred_element_type=f32)
    part = total.astype(bf16)
    for target in range(part_ref.shape[0]):
        part_ref[target] = part
    for copy in leaving:
        copy.wait()


def qkv_kernel(parts_ref, rows_ref, gain_ref, wq_ref, wk_ref, wv_ref, residual_ref, out_ref):
    total = parts_ref[0].astype(f32)
    for source in range(1, parts_ref.shape[0]):
        total = total + parts_ref[source].astype(f32)
    residual = rows_ref[...].astype(f32) + total
    residual_ref[...] = residual
    scaled = (residual * gain_ref[...]).astype(bf16)
    column = jnp.sum(residual * residual, axis=1, keepdims=True)
    at = 0
    for weight_ref in (wq_ref, wk_ref, wv_ref):
        width = weight_ref.shape[1]
        out_ref[:, at : at + width] = jnp.dot(
            scaled, weight_ref[...], preferred_element_type=f32
        ).astype(bf16)
        at += width
    out_ref[:, at:] = pair_columns(column).astype(bf16)


def pair_columns(column):
    hi = rounded(column)
    which = lane_index(ALL_ROWS)
    return jnp.where(which == 0, hi, jnp.where(which == 1, column - hi, 0.0))


def sum_refs(refs):
    parts = [ref[...].astype(f32) for ref in refs]
    if len(parts) == 2:
        return parts[0] + parts[1]
    return (parts[0] + parts[1]) + (parts[2] + parts[3])


def qkv_sum_kernel(*refs):
    out_ref = refs[-1]
    total = sum_refs(refs[:-1])
    column = jnp.sum(total[:, -LANES:], axis=1, keepdims=True)
    out_ref[:, :-LANES] = total[:, :-LANES].astype(bf16)
    out_ref[:, -LANES:] = pair_columns(column).astype(bf16)


def pack_logs(logs):
    which = lane_index(ALL_ROWS)
    logs = jnp.where(which < ROWS, logs, 0.0)
    hi = rounded(logs)
    mid = rounded(logs - hi)
    low = logs - hi - mid
    return hi + pltpu.roll(mid, ROWS, 1) + pltpu.roll(low, 2 * ROWS, 1)


def unpack_logs(packed):
    return (
        packed + pltpu.roll(packed, LANES - ROWS, 1) + pltpu.roll(packed, LANES - 2 * ROWS, 1)
    )


def attention_kernel(
    width_all, first_ref, lengths_ref, blocks_ref, own_ref, one_ref, two_ref, three_ref,
    keys_ref, values_ref,
    new_keys_ref, new_values_ref, out_ref, query, fresh_k, fresh_v,
):
    total = sum_refs((own_ref, one_ref, two_ref, three_ref))
    column = jnp.sum(total[:, -LANES:], axis=1, keepdims=True)
    total = rounded(total[:, :-LANES] * lax.rsqrt(column / width_all + 1e-06))
    heads = total.shape[1] // HEAD - 2
    queries = STEPS * heads
    keys_now = total[:, heads * HEAD : (heads + 1) * HEAD]
    values_now = total[:, (heads + 1) * HEAD :]
    new_keys_ref[...] = keys_now.astype(bf16)
    new_values_ref[...] = values_now.astype(bf16)
    fresh_k[...] = jnp.zeros_like(fresh_k)
    fresh_v[...] = jnp.zeros_like(fresh_v)
    for s in range(STEPS):
        rows = slice(s * ROWS, (s + 1) * ROWS)
        fresh_k[pl.ds(s, ROWS, stride=8), :] = keys_now[rows]
        fresh_v[pl.ds(s, ROWS, stride=8), :] = values_now[rows]
        for g in range(heads):
            query[pl.ds(s * heads + g, ROWS, stride=queries), :] = total[
                rows, g * HEAD : (g + 1) * HEAD
            ]
    which = lane_index(queries, 8)
    fresh_live = (which * heads <= row_index(queries, 8)) & (which < STEPS)
    fresh_live = fresh_live & (first_ref[0] == 1)
    score_scale = HEAD**-0.5
    lanes = lane_index(queries)
    contract = (((1,), (1,)), ((), ()))
    every = range(ROWS)
    scores, fresh, live = [], [], []
    for b in every:
        query_b = query[b * queries : (b + 1) * queries, :].astype(bf16)
        scores.append(
            lax.dot_general(query_b, keys_ref[b], contract, preferred_element_type=f32)
        )
        fresh.append(
            lax.dot_general(
                query_b,
                fresh_k[b * 8 : (b + 1) * 8, :].astype(bf16),
                contract,
                preferred_element_type=f32,
            )
        )
        live.append(
            jnp.concatenate(
                [
                    lanes < lengths_ref[b] - blocks_ref[k, b] * BLK
                    for k in range(keys_ref.shape[1] // BLK)
                ],
                axis=1,
            )
        )
    scores = [jnp.where(live[b], scores[b] * score_scale, NEGATIVE) for b in every]
    fresh = [jnp.where(fresh_live, fresh[b] * score_scale, NEGATIVE) for b in every]
    peaks = [
        jnp.maximum(
            jnp.max(scores[b], axis=1, keepdims=True), jnp.max(fresh[b], axis=1, keepdims=True)
        )
        for b in every
    ]
    weights = [jnp.where(live[b], jnp.exp(scores[b] - peaks[b]), 0.0) for b in every]
    fresh = [jnp.where(fresh_live, jnp.exp(fresh[b] - peaks[b]), 0.0) for b in every]
    attended = [
        jnp.dot(weights[b].astype(bf16), values_ref[b], preferred_element_type=f32)
        + jnp.dot(
            fresh[b].astype(bf16),
            fresh_v[b * 8 : (b + 1) * 8, :].astype(bf16),
            preferred_element_type=f32,
        )
        for b in every
    ]
    sums = [
        jnp.sum(weights[b], axis=1, keepdims=True) + jnp.sum(fresh[b], axis=1, keepdims=True)
        for b in every
    ]
    logs = jnp.zeros((queries, LANES), f32)
    for b in every:
        any_live = sums[b] > 0
        safe = jnp.where(any_live, sums[b], 1.0)
        out_ref[b] = (attended[b] / safe).astype(bf16)
        log_sum = jnp.where(any_live, peaks[b] + jnp.log(safe), NEGATIVE)
        logs = jnp.where(lanes == b, log_sum, logs)
    out_ref[ROWS] = pack_logs(logs).astype(bf16)


def shares_of(refs):
    logs = [unpack_logs(ref[ROWS].astype(f32)) for ref in refs]
    top = functools.reduce(jnp.maximum, logs)
    shares = [jnp.exp(log - top) for log in logs]
    total = functools.reduce(jnp.add, shares)
    return [share / total for share in shares], top + jnp.log(total)


def combined_row(refs, shares, b):
    attended = [shares[i][:, b : b + 1] * ref[b].astype(f32) for i, ref in enumerate(refs)]
    return functools.reduce(jnp.add, attended)


def combine_kernel(*refs):
    refs, out_ref = refs[:-1], refs[-1]
    shares, logs = shares_of(refs)
    for b in range(ROWS):
        out_ref[b] = combined_row(refs, shares, b).astype(bf16)
    out_ref[ROWS] = pack_logs(logs).astype(bf16)


def finish_kernel(own_ref, one_ref, two_ref, three_ref, weight_ref, out_ref, attended):
    refs = (own_ref, one_ref, two_ref, three_ref)
    shares, _ = shares_of(refs)
    for b in range(ROWS):
        queries = shares[0].shape[0]
        attended[b * queries : (b + 1) * queries, :] = combined_row(refs, shares, b)
    heads = queries // STEPS
    rows = jnp.concatenate(
        [
            jnp.concatenate(
                [
                    attended[pl.ds(s * heads + g, ROWS, stride=queries), :]
                    for g in range(heads)
                ],
                axis=1,
            )
            for s in range(STEPS)
        ],
        axis=0,
    ).astype(bf16)
    part = jnp.dot(rows, weight_ref[...], preferred_element_type=f32).astype(bf16)
    out_ref[...] = part


def body(
    embeds, norm_mamba, in_x, in_z, conv_w, conv_b, x_proj, dt_norm, b_norm, c_norm, dt_proj,
    dt_bias, a_log, d_skip, out_proj, norm_attn, w_query, key_matrix, value_matrix, w_out,
    cache_k, value_cache, lengths, block_of_slot, conv_state, ssm_state,
):
    ctx_size, tp_size = (lax.axis_size(axis) for axis in (CTX, TP))
    local_width = embeds.shape[2]
    width_all = float(local_width * ctx_size)
    channels = in_x.shape[1]
    heads = w_query.shape[1] // HEAD
    queries = STEPS * heads
    chunk_count = channels // LANES
    rows_in = embeds.reshape(ALL_ROWS, local_width)

    hbm = pl.BlockSpec(memory_space=pltpu.HBM)
    vmem = pl.BlockSpec(memory_space=pltpu.VMEM)
    (chunks,) = call(
        project_kernel,
        [((2, chunk_count, 32, LANES), bf16)],
        rows_in,
        norm_mamba.reshape(1, -1),
        in_x,
        in_z,
        vmem_mib=62,
        in_specs=[hbm] * 4,
        scratch_shapes=[
            pltpu.VMEM((ALL_ROWS, local_width), bf16),
            pltpu.VMEM((1, local_width), f32),
            pltpu.VMEM(in_x.shape, bf16),
            pltpu.VMEM(in_z.shape, bf16),
            pltpu.SemaphoreType.DMA((2,)),
            pltpu.SemaphoreType.DMA((2,)),
        ],
    )
    received = exchange(chunks.reshape(2 * chunk_count, 32, LANES), CTX)
    (mine,) = call(
        functools.partial(reduce_kernel, width_all),
        [((ctx_size, ALL_ROWS, LANES), bf16)],
        received,
    )
    inner = exchange(mine, CTX)

    low, mixed, history = call(
        conv_kernel,
        [
            ((ALL_ROWS, DTR + 2 * DS), bf16),
            ((ALL_ROWS, channels), f32),
            ((STEPS, ROWS, channels), f32),
        ],
        inner,
        conv_state.transpose(1, 0, 2),
        conv_w,
        conv_b.reshape(1, -1),
        x_proj.T,
        scratch_shapes=[pltpu.VMEM((ALL_ROWS, channels), bf16)],
    )
    low = over_cores(low)
    tiled = (chunk_count, DS, ROWS, LANES)
    state = ssm_state.reshape(ROWS, DS, chunk_count, LANES).transpose(2, 1, 0, 3)
    state, part = call(
        scan_kernel,
        [(tiled, f32), ((tp_size, ALL_ROWS, local_width), bf16)],
        low,
        *from_partners(low, "y"),
        dt_norm.reshape(1, -1),
        b_norm.reshape(1, -1),
        c_norm.reshape(1, -1),
        dt_bias.reshape(1, -1),
        a_log,
        d_skip.reshape(1, -1),
        mixed,
        inner,
        state,
        dt_proj,
        out_proj,
        vmem_mib=53,
        in_specs=[vmem] * 12 + [hbm] * 3,
        out_specs=[hbm, vmem],
        scratch_shapes=[
            pltpu.VMEM(dt_proj.shape, bf16),
            pltpu.VMEM(out_proj.shape, bf16),
            pltpu.VMEM(tiled, f32),
            pltpu.VMEM((DS, ALL_ROWS, LANES), f32),
            pltpu.VMEM((DS, ALL_ROWS, LANES), f32),
            pltpu.VMEM(tiled, f32),
            pltpu.SemaphoreType.DMA((2,)),
            pltpu.SemaphoreType.DMA((2, GROUPS)),
        ],
    )
    state = state.transpose(2, 1, 0, 3).reshape(ssm_state.shape)
    part = exchange(part, TP)

    packed_width = (heads + 3) * HEAD
    residual, projected = call(
        qkv_kernel,
        [((ALL_ROWS, local_width), f32), ((ALL_ROWS, packed_width), bf16)],
        part,
        rows_in,
        norm_attn.reshape(1, -1),
        w_query,
        key_matrix,
        value_matrix,
    )
    shape = ((ALL_ROWS, packed_width), bf16)
    (projected,) = call(qkv_sum_kernel, [shape], projected, *from_partners(projected))
    (projected,) = call(qkv_sum_kernel, [shape], projected, from_other(projected, "zb"))
    others = from_partners(projected, "za")
    *others, state = lax.optimization_barrier((*others, state))

    first = (lax.axis_index(CTX) == 0).astype(jnp.int32).reshape(1)
    new_keys, new_values, attended = call(
        functools.partial(attention_kernel, width_all),
        [
            ((ALL_ROWS, HEAD), bf16),
            ((ALL_ROWS, HEAD), bf16),
            ((ROWS + 1, queries, HEAD), bf16),
        ],
        first,
        lengths,
        block_of_slot.T,
        projected,
        *others,
        cache_k,
        value_cache,
        in_specs=[pl.BlockSpec(memory_space=pltpu.SMEM)] * 3 + [vmem] * 6,
        scratch_shapes=[
            pltpu.VMEM((ROWS * queries, HEAD), f32),
            pltpu.VMEM((ROWS * 8, HEAD), f32),
            pltpu.VMEM((ROWS * 8, HEAD), f32),
        ],
    )
    shape = (attended.shape, bf16)
    (attended,) = call(combine_kernel, [shape], attended, *from_partners(attended))
    (attended,) = call(combine_kernel, [shape], attended, from_other(attended, "zb"))
    (part,) = call(
        finish_kernel,
        [((ALL_ROWS, local_width), bf16)],
        attended,
        *from_partners(attended, "za"),
        w_out,
        scratch_shapes=[pltpu.VMEM((ROWS * queries, HEAD), f32)],
    )
    part = over_cores(part)
    one, two, three = (other.astype(f32) for other in from_partners(part, "y"))
    hidden = residual + ((part.astype(f32) + one) + (two + three))
    return (
        hidden.reshape(STEPS, ROWS, local_width),
        new_keys.reshape(STEPS, ROWS, HEAD),
        new_values.reshape(STEPS, ROWS, HEAD),
        state,
        history.transpose(1, 0, 2),
    )


def solution(mesh):
    ctx_size, tp_size = mesh.devices.shape
    split = Mesh(
        mesh.devices.reshape(ctx_size // X_SIZE // 2, 2, X_SIZE, tp_size // 2, 2),
        ("za", "zb", "x", "y", "core"),
    )
    return jax.shard_map(
        body,
        mesh=split,
        in_specs=(
            P(None, None, CTX),
            P(CTX),
            P(CTX, TP),
            P(CTX, TP),
            P(None, TP),
            P(TP),
            P(TP, None),
            P(),
            P(),
            P(),
            P(None, TP),
            P(TP),
            P(None, TP),
            P(TP),
            P(TP, CTX),
            P(CTX),
            P(CTX, TP),
            P(CTX, TP),
            P(CTX, TP),
            P(TP, CTX),
            P(None, CTX, TP),
            P(None, CTX, TP),
            P(),
            P(None, CTX),
            P(None, None, TP),
            P(None, None, TP),
        ),
        out_specs=(
            P(None, None, CTX),
            P(None, None, TP),
            P(None, None, TP),
            P(None, None, TP),
            P(None, None, TP),
        ),
        check_vma=False,
    )
```

```python
import functools

import jax
import jax.numpy as jnp
from jax import lax
from jax.experimental import pallas as pl
from jax.experimental.pallas import tpu as pltpu
from jax.sharding import Mesh, PartitionSpec as P

DS = 16
DTR = 512
HEAD = 128
BLK = 128
STEPS = 3
ROWS = 8
ALL_ROWS = STEPS * ROWS
LANES = 128
X_SIZE = 4
CTX = ("za", "zb", "x")
TP = ("y", "core")
FLOPS = 3_000_000_000
NEGATIVE = -1e30
bf16 = jnp.bfloat16
f32 = jnp.float32


def exchange(parts, axis):
    return lax.all_to_all(parts, axis, 0, 0, tiled=True)


def from_partners(part, axis="x"):
    received = {
        flip: lax.ppermute(part, axis, [(i, i ^ flip) for i in range(4)]) for flip in (1, 3, 2)
    }
    return received[1], received[2], received[3]


def from_other(part, axis):
    return lax.ppermute(part, axis, [(0, 1), (1, 0)])


def over_cores(part):
    return part + from_other(part, "core")


def call(kernel, outs, *operands, vmem_mib=48, **options):
    return pl.pallas_call(
        kernel,
        out_shape=[jax.ShapeDtypeStruct(shape, dtype) for shape, dtype in outs],
        compiler_params=pltpu.CompilerParams(vmem_limit_bytes=vmem_mib * 1024 * 1024),
        cost_estimate=pl.CostEstimate(flops=FLOPS, bytes_accessed=8 << 20, transcendentals=0),
        **options,
    )(*operands)


def lane_index(rows, lanes=LANES):
    return lax.broadcasted_iota(jnp.int32, (rows, lanes), 1)


def row_index(rows, lanes=LANES):
    return lax.broadcasted_iota(jnp.int32, (rows, lanes), 0)


def rounded(value):
    return value.astype(bf16).astype(f32)


def silu(value):
    return value / (1.0 + jnp.exp(-value))


def project_kernel(
    rows_hbm, gain_hbm, wx_hbm, wz_hbm, out_ref, rows_ref, gain_ref, wx_ref, wz_ref, sems, small_sems
):
    small = [
        pltpu.make_async_copy(rows_hbm, rows_ref, small_sems.at[0]),
        pltpu.make_async_copy(gain_hbm, gain_ref, small_sems.at[1]),
    ]
    for copy in small:
        copy.start()
    copies = []
    for half, (source, target) in enumerate(((wx_hbm, wx_ref), (wz_hbm, wz_ref))):
        copies.append(pltpu.make_async_copy(source, target, sems.at[half]))
        copies[-1].start()
    for copy in small:
        copy.wait()
    rows = rows_ref[...].astype(f32)
    scaled = (rows * gain_ref[...]).astype(bf16)
    column = jnp.sum(rows * rows, axis=1, keepdims=True)
    eye = row_index(ALL_ROWS) == lane_index(ALL_ROWS)
    squares = jnp.sum(jnp.where(eye, column, 0.0), axis=0, keepdims=True)
    hi = rounded(squares)
    which = row_index(8)
    stats = jnp.where(which == 0, hi, jnp.where(which == 1, squares - hi, 0.0))
    for half, weight_ref in enumerate((wx_ref, wz_ref)):
        copies[half].wait()
        part = jnp.dot(scaled, weight_ref[...], preferred_element_type=f32)
        for k in range(out_ref.shape[1]):
            chunk = part[:, k * LANES : (k + 1) * LANES]
            out_ref[half, k] = jnp.concatenate([chunk, stats], axis=0).astype(bf16)


def reduce_kernel(width_all, in_ref, out_ref):
    total = in_ref[0].astype(f32)
    for source in range(1, in_ref.shape[0]):
        total = total + in_ref[source].astype(f32)
    squares = total[ALL_ROWS : ALL_ROWS + 1] + total[ALL_ROWS + 1 : ALL_ROWS + 2]
    eye = row_index(ALL_ROWS) == lane_index(ALL_ROWS)
    column = jnp.sum(jnp.where(eye, squares, 0.0), axis=1, keepdims=True)
    mine = (total[:ALL_ROWS] * lax.rsqrt(column / width_all + 1e-06)).astype(bf16)
    for target in range(out_ref.shape[0]):
        out_ref[target] = mine


def conv_kernel(inner_ref, hist_ref, taps_ref, bias_ref, xp_ref, low_ref, mixed_ref, hist_out_ref, mixed16):
    for k in range(mixed_ref.shape[1] // LANES):
        cols = slice(k * LANES, (k + 1) * LANES)
        fresh = inner_ref[k].astype(f32)
        window = [hist_ref[t, :, cols] for t in range(STEPS)]
        window += [fresh[s * ROWS : (s + 1) * ROWS] for s in range(STEPS)]
        taps = taps_ref[:, cols]
        bias = bias_ref[:, cols]
        mixed = []
        for s in range(STEPS):
            total = window[s] * taps[0:1]
            for t in range(1, STEPS + 1):
                total = total + window[s + t] * taps[t : t + 1]
            mixed.append(silu(total + bias))
            hist_out_ref[s, :, cols] = window[STEPS + s]
        mixed = jnp.concatenate(mixed, axis=0)
        mixed_ref[:, cols] = mixed
        mixed16[:, cols] = mixed.astype(bf16)
    low = lax.dot_general(
        mixed16[...], xp_ref[...], (((1,), (1,)), ((), ())), preferred_element_type=f32
    ).astype(bf16)
    low_ref[...] = low


def scan_kernel(
    own_ref, one_ref, two_ref, three_ref, dt_gain_ref, b_gain_ref, c_gain_ref, dt_bias_ref, a_ref, skip_ref, mixed_ref, gate_ref,
    state_ref, dtp_ref, op_ref, state_out_ref, part_ref, b_wide, c_wide, decay_wide,
):
    tiles = state_ref.shape[0]
    low = sum_refs((own_ref, one_ref, two_ref, three_ref))
    raw = low[:, :DTR]
    mean_sq = jnp.sum(raw * raw, axis=1, keepdims=True) / DTR
    dt_low = (raw * lax.rsqrt(mean_sq + 1e-06) * dt_gain_ref[...]).astype(bf16)
    for wide, gain_ref, at in ((b_wide, b_gain_ref, DTR), (c_wide, c_gain_ref, DTR + DS)):
        raw = low[:, at : at + DS]
        mean_sq = jnp.sum(raw * raw, axis=1, keepdims=True) / DS
        normed = raw * lax.rsqrt(mean_sq + 1e-06) * gain_ref[...]
        for n in range(DS):
            wide[n] = jnp.broadcast_to(normed[:, n : n + 1], (ALL_ROWS, LANES))
    for tile in range(tiles):
        decay = -jnp.exp(a_ref[:, tile * LANES : (tile + 1) * LANES])
        for n in range(DS):
            decay_wide[tile, n] = jnp.broadcast_to(decay[n : n + 1], (ROWS, LANES))
    raw = jnp.dot(dt_low, dtp_ref[...], preferred_element_type=f32) + dt_bias_ref[...]
    steps = jnp.maximum(raw, 0.0) + jnp.log1p(jnp.exp(-jnp.abs(raw)))
    mixed = mixed_ref[...]
    drive = steps * mixed
    scanned = []
    for tile in range(tiles):
        cols = slice(tile * LANES, (tile + 1) * LANES)
        y = [jnp.zeros((ROWS, LANES), f32) for _ in range(STEPS)]
        for n in range(DS):
            state = state_ref[tile, n]
            decay = decay_wide[tile, n]
            for s in range(STEPS):
                rows = slice(s * ROWS, (s + 1) * ROWS)
                state = (
                    jnp.exp(steps[rows, cols] * decay) * state + drive[rows, cols] * b_wide[n, rows]
                )
                y[s] = y[s] + c_wide[n, rows] * state
            state_out_ref[tile, n] = state
        y = jnp.concatenate(y, axis=0) + skip_ref[:, cols] * mixed[:, cols]
        scanned.append((y * silu(gate_ref[tiles + tile].astype(f32))).astype(bf16))
    total = jnp.dot(jnp.concatenate(scanned, axis=1), op_ref[...], preferred_element_type=f32)
    part = total.astype(bf16)
    for target in range(part_ref.shape[0]):
        part_ref[target] = part


def qkv_kernel(parts_ref, rows_ref, gain_ref, wq_ref, wk_ref, wv_ref, residual_ref, out_ref):
    total = parts_ref[0].astype(f32)
    for source in range(1, parts_ref.shape[0]):
        total = total + parts_ref[source].astype(f32)
    residual = rows_ref[...].astype(f32) + total
    residual_ref[...] = residual
    scaled = (residual * gain_ref[...]).astype(bf16)
    column = jnp.sum(residual * residual, axis=1, keepdims=True)
    at = 0
    for weight_ref in (wq_ref, wk_ref, wv_ref):
        width = weight_ref.shape[1]
        out_ref[:, at : at + width] = jnp.dot(
            scaled, weight_ref[...], preferred_element_type=f32
        ).astype(bf16)
        at += width
    out_ref[:, at:] = pair_columns(column).astype(bf16)


def pair_columns(column):
    hi = rounded(column)
    which = lane_index(ALL_ROWS)
    return jnp.where(which == 0, hi, jnp.where(which == 1, column - hi, 0.0))


def sum_refs(refs):
    parts = [ref[...].astype(f32) for ref in refs]
    if len(parts) == 2:
        return parts[0] + parts[1]
    return (parts[0] + parts[1]) + (parts[2] + parts[3])


def qkv_sum_kernel(*refs):
    out_ref = refs[-1]
    total = sum_refs(refs[:-1])
    column = jnp.sum(total[:, -LANES:], axis=1, keepdims=True)
    out_ref[:, :-LANES] = total[:, :-LANES].astype(bf16)
    out_ref[:, -LANES:] = pair_columns(column).astype(bf16)


def pack_logs(logs):
    which = lane_index(ALL_ROWS)
    logs = jnp.where(which < ROWS, logs, 0.0)
    hi = rounded(logs)
    mid = rounded(logs - hi)
    low = logs - hi - mid
    return hi + pltpu.roll(mid, ROWS, 1) + pltpu.roll(low, 2 * ROWS, 1)


def unpack_logs(packed):
    return (
        packed + pltpu.roll(packed, LANES - ROWS, 1) + pltpu.roll(packed, LANES - 2 * ROWS, 1)
    )


def attention_kernel(
    width_all, first_ref, lengths_ref, blocks_ref, own_ref, one_ref, two_ref, three_ref,
    keys_ref, values_ref,
    new_keys_ref, new_values_ref, out_ref, query, fresh_k, fresh_v,
):
    total = sum_refs((own_ref, one_ref, two_ref, three_ref))
    column = jnp.sum(total[:, -LANES:], axis=1, keepdims=True)
    total = rounded(total[:, :-LANES] * lax.rsqrt(column / width_all + 1e-06))
    heads = total.shape[1] // HEAD - 2
    queries = STEPS * heads
    keys_now = total[:, heads * HEAD : (heads + 1) * HEAD]
    values_now = total[:, (heads + 1) * HEAD :]
    new_keys_ref[...] = keys_now.astype(bf16)
    new_values_ref[...] = values_now.astype(bf16)
    fresh_k[...] = jnp.zeros_like(fresh_k)
    fresh_v[...] = jnp.zeros_like(fresh_v)
    for s in range(STEPS):
        rows = slice(s * ROWS, (s + 1) * ROWS)
        fresh_k[pl.ds(s, ROWS, stride=8), :] = keys_now[rows]
        fresh_v[pl.ds(s, ROWS, stride=8), :] = values_now[rows]
        for g in range(heads):
            query[pl.ds(s * heads + g, ROWS, stride=queries), :] = total[
                rows, g * HEAD : (g + 1) * HEAD
            ]
    which = lane_index(queries, 8)
    fresh_live = (which * heads <= row_index(queries, 8)) & (which < STEPS)
    fresh_live = fresh_live & (first_ref[0] == 1)
    score_scale = HEAD**-0.5
    lanes = lane_index(queries)
    contract = (((1,), (1,)), ((), ()))
    every = range(ROWS)
    scores, fresh, live = [], [], []
    for b in every:
        query_b = query[b * queries : (b + 1) * queries, :].astype(bf16)
        scores.append(
            lax.dot_general(query_b, keys_ref[b], contract, preferred_element_type=f32)
        )
        fresh.append(
            lax.dot_general(
                query_b,
                fresh_k[b * 8 : (b + 1) * 8, :].astype(bf16),
                contract,
                preferred_element_type=f32,
            )
        )
        live.append(
            jnp.concatenate(
                [
                    lanes < lengths_ref[b] - blocks_ref[k, b] * BLK
                    for k in range(keys_ref.shape[1] // BLK)
                ],
                axis=1,
            )
        )
    scores = [jnp.where(live[b], scores[b] * score_scale, NEGATIVE) for b in every]
    fresh = [jnp.where(fresh_live, fresh[b] * score_scale, NEGATIVE) for b in every]
    peaks = [
        jnp.maximum(
            jnp.max(scores[b], axis=1, keepdims=True), jnp.max(fresh[b], axis=1, keepdims=True)
        )
        for b in every
    ]
    weights = [jnp.where(live[b], jnp.exp(scores[b] - peaks[b]), 0.0) for b in every]
    fresh = [jnp.where(fresh_live, jnp.exp(fresh[b] - peaks[b]), 0.0) for b in every]
    attended = [
        jnp.dot(weights[b].astype(bf16), values_ref[b], preferred_element_type=f32)
        + jnp.dot(
            fresh[b].astype(bf16),
            fresh_v[b * 8 : (b + 1) * 8, :].astype(bf16),
            preferred_element_type=f32,
        )
        for b in every
    ]
    sums = [
        jnp.sum(weights[b], axis=1, keepdims=True) + jnp.sum(fresh[b], axis=1, keepdims=True)
        for b in every
    ]
    logs = jnp.zeros((queries, LANES), f32)
    for b in every:
        any_live = sums[b] > 0
        safe = jnp.where(any_live, sums[b], 1.0)
        out_ref[b] = (attended[b] / safe).astype(bf16)
        log_sum = jnp.where(any_live, peaks[b] + jnp.log(safe), NEGATIVE)
        logs = jnp.where(lanes == b, log_sum, logs)
    out_ref[ROWS] = pack_logs(logs).astype(bf16)


def shares_of(refs):
    logs = [unpack_logs(ref[ROWS].astype(f32)) for ref in refs]
    top = functools.reduce(jnp.maximum, logs)
    shares = [jnp.exp(log - top) for log in logs]
    total = functools.reduce(jnp.add, shares)
    return [share / total for share in shares], top + jnp.log(total)


def combined_row(refs, shares, b):
    attended = [shares[i][:, b : b + 1] * ref[b].astype(f32) for i, ref in enumerate(refs)]
    return functools.reduce(jnp.add, attended)


def combine_kernel(*refs):
    refs, out_ref = refs[:-1], refs[-1]
    shares, logs = shares_of(refs)
    for b in range(ROWS):
        out_ref[b] = combined_row(refs, shares, b).astype(bf16)
    out_ref[ROWS] = pack_logs(logs).astype(bf16)


def finish_kernel(own_ref, one_ref, two_ref, three_ref, weight_ref, out_ref, attended):
    refs = (own_ref, one_ref, two_ref, three_ref)
    shares, _ = shares_of(refs)
    for b in range(ROWS):
        queries = shares[0].shape[0]
        attended[b * queries : (b + 1) * queries, :] = combined_row(refs, shares, b)
    heads = queries // STEPS
    rows = jnp.concatenate(
        [
            jnp.concatenate(
                [
                    attended[pl.ds(s * heads + g, ROWS, stride=queries), :]
                    for g in range(heads)
                ],
                axis=1,
            )
            for s in range(STEPS)
        ],
        axis=0,
    ).astype(bf16)
    part = jnp.dot(rows, weight_ref[...], preferred_element_type=f32).astype(bf16)
    out_ref[...] = part


def body(
    embeds, norm_mamba, in_x, in_z, conv_w, conv_b, x_proj, dt_norm, b_norm, c_norm, dt_proj,
    dt_bias, a_log, d_skip, out_proj, norm_attn, w_query, key_matrix, value_matrix, w_out,
    cache_k, value_cache, lengths, block_of_slot, conv_state, ssm_state,
):
    ctx_size, tp_size = (lax.axis_size(axis) for axis in (CTX, TP))
    local_width = embeds.shape[2]
    width_all = float(local_width * ctx_size)
    channels = in_x.shape[1]
    heads = w_query.shape[1] // HEAD
    queries = STEPS * heads
    chunk_count = channels // LANES
    rows_in = embeds.reshape(ALL_ROWS, local_width)

    hbm = pl.BlockSpec(memory_space=pltpu.HBM)
    vmem = pl.BlockSpec(memory_space=pltpu.VMEM)
    (chunks,) = call(
        project_kernel,
        [((2, chunk_count, 32, LANES), bf16)],
        rows_in,
        norm_mamba.reshape(1, -1),
        in_x,
        in_z,
        vmem_mib=62,
        in_specs=[hbm] * 4,
        scratch_shapes=[
            pltpu.VMEM((ALL_ROWS, local_width), bf16),
            pltpu.VMEM((1, local_width), f32),
            pltpu.VMEM(in_x.shape, bf16),
            pltpu.VMEM(in_z.shape, bf16),
            pltpu.SemaphoreType.DMA((2,)),
            pltpu.SemaphoreType.DMA((2,)),
        ],
    )
    received = exchange(chunks.reshape(2 * chunk_count, 32, LANES), CTX)
    (mine,) = call(
        functools.partial(reduce_kernel, width_all),
        [((ctx_size, ALL_ROWS, LANES), bf16)],
        received,
    )
    inner = exchange(mine, CTX)

    low, mixed, history = call(
        conv_kernel,
        [
            ((ALL_ROWS, DTR + 2 * DS), bf16),
            ((ALL_ROWS, channels), f32),
            ((STEPS, ROWS, channels), f32),
        ],
        inner,
        conv_state.transpose(1, 0, 2),
        conv_w,
        conv_b.reshape(1, -1),
        x_proj.T,
        scratch_shapes=[pltpu.VMEM((ALL_ROWS, channels), bf16)],
    )
    low = over_cores(low)
    tiled = (chunk_count, DS, ROWS, LANES)
    state = ssm_state.reshape(ROWS, DS, chunk_count, LANES).transpose(2, 1, 0, 3)
    state, part = call(
        scan_kernel,
        [(tiled, f32), ((tp_size, ALL_ROWS, local_width), bf16)],
        low,
        *from_partners(low, "y"),
        dt_norm.reshape(1, -1),
        b_norm.reshape(1, -1),
        c_norm.reshape(1, -1),
        dt_bias.reshape(1, -1),
        a_log,
        d_skip.reshape(1, -1),
        mixed,
        inner,
        state,
        dt_proj,
        out_proj,
        scratch_shapes=[
            pltpu.VMEM((DS, ALL_ROWS, LANES), f32),
            pltpu.VMEM((DS, ALL_ROWS, LANES), f32),
            pltpu.VMEM(tiled, f32),
        ],
    )
    state = state.transpose(2, 1, 0, 3).reshape(ssm_state.shape)
    part = exchange(part, TP)

    packed_width = (heads + 3) * HEAD
    residual, projected = call(
        qkv_kernel,
        [((ALL_ROWS, local_width), f32), ((ALL_ROWS, packed_width), bf16)],
        part,
        rows_in,
        norm_attn.reshape(1, -1),
        w_query,
        key_matrix,
        value_matrix,
    )
    shape = ((ALL_ROWS, packed_width), bf16)
    (projected,) = call(qkv_sum_kernel, [shape], projected, *from_partners(projected))
    (projected,) = call(qkv_sum_kernel, [shape], projected, from_other(projected, "zb"))
    others = from_partners(projected, "za")
    *others, state = lax.optimization_barrier((*others, state))

    first = (lax.axis_index(CTX) == 0).astype(jnp.int32).reshape(1)
    new_keys, new_values, attended = call(
        functools.partial(attention_kernel, width_all),
        [
            ((ALL_ROWS, HEAD), bf16),
            ((ALL_ROWS, HEAD), bf16),
            ((ROWS + 1, queries, HEAD), bf16),
        ],
        first,
        lengths,
        block_of_slot.T,
        projected,
        *others,
        cache_k,
        value_cache,
        in_specs=[pl.BlockSpec(memory_space=pltpu.SMEM)] * 3 + [vmem] * 6,
        scratch_shapes=[
            pltpu.VMEM((ROWS * queries, HEAD), f32),
            pltpu.VMEM((ROWS * 8, HEAD), f32),
            pltpu.VMEM((ROWS * 8, HEAD), f32),
        ],
    )
    shape = (attended.shape, bf16)
    (attended,) = call(combine_kernel, [shape], attended, *from_partners(attended))
    (attended,) = call(combine_kernel, [shape], attended, from_other(attended, "zb"))
    (part,) = call(
        finish_kernel,
        [((ALL_ROWS, local_width), bf16)],
        attended,
        *from_partners(attended, "za"),
        w_out,
        scratch_shapes=[pltpu.VMEM((ROWS * queries, HEAD), f32)],
    )
    part = over_cores(part)
    one, two, three = (other.astype(f32) for other in from_partners(part, "y"))
    hidden = residual + ((part.astype(f32) + one) + (two + three))
    return (
        hidden.reshape(STEPS, ROWS, local_width),
        new_keys.reshape(STEPS, ROWS, HEAD),
        new_values.reshape(STEPS, ROWS, HEAD),
        state,
        history.transpose(1, 0, 2),
    )


def solution(mesh):
    ctx_size, tp_size = mesh.devices.shape
    split = Mesh(
        mesh.devices.reshape(ctx_size // X_SIZE // 2, 2, X_SIZE, tp_size // 2, 2),
        ("za", "zb", "x", "y", "core"),
    )
    return jax.shard_map(
        body,
        mesh=split,
        in_specs=(
            P(None, None, CTX),
            P(CTX),
            P(CTX, TP),
            P(CTX, TP),
            P(None, TP),
            P(TP),
            P(TP, None),
            P(),
            P(),
            P(),
            P(None, TP),
            P(TP),
            P(None, TP),
            P(TP),
            P(TP, CTX),
            P(CTX),
            P(CTX, TP),
            P(CTX, TP),
            P(CTX, TP),
            P(TP, CTX),
            P(None, CTX, TP),
            P(None, CTX, TP),
            P(),
            P(None, CTX),
            P(None, None, TP),
            P(None, None, TP),
        ),
        out_specs=(
            P(None, None, CTX),
            P(None, None, TP),
            P(None, None, TP),
            P(None, None, TP),
            P(None, None, TP),
        ),
        check_vma=False,
    )
```

```python
import functools

import jax
import jax.numpy as jnp
from jax import lax
from jax.experimental import pallas as pl
from jax.experimental.pallas import tpu as pltpu
from jax.sharding import Mesh, PartitionSpec as P

DS = 16
DTR = 512
HEAD = 128
BLK = 128
STEPS = 3
ROWS = 8
ALL_ROWS = STEPS * ROWS
LANES = 128
X_SIZE = 4
CTX = ("za", "zb", "x")
TP = ("y", "core")
FLOPS = 3_000_000_000
NEGATIVE = -1e30
bf16 = jnp.bfloat16
f32 = jnp.float32


def exchange(parts, axis):
    return lax.all_to_all(parts, axis, 0, 0, tiled=True)


def from_partners(part, axis="x"):
    received = {
        flip: lax.ppermute(part, axis, [(i, i ^ flip) for i in range(4)]) for flip in (1, 3, 2)
    }
    return received[1], received[2], received[3]


def from_other(part, axis):
    return lax.ppermute(part, axis, [(0, 1), (1, 0)])


def over_cores(part):
    return part + from_other(part, "core")


def call(kernel, outs, *operands, vmem_mib=48, **options):
    return pl.pallas_call(
        kernel,
        out_shape=[jax.ShapeDtypeStruct(shape, dtype) for shape, dtype in outs],
        compiler_params=pltpu.CompilerParams(vmem_limit_bytes=vmem_mib * 1024 * 1024),
        cost_estimate=pl.CostEstimate(flops=FLOPS, bytes_accessed=8 << 20, transcendentals=0),
        **options,
    )(*operands)


def lane_index(rows, lanes=LANES):
    return lax.broadcasted_iota(jnp.int32, (rows, lanes), 1)


def row_index(rows, lanes=LANES):
    return lax.broadcasted_iota(jnp.int32, (rows, lanes), 0)


def rounded(value):
    return value.astype(bf16).astype(f32)


def silu(value):
    return value / (1.0 + jnp.exp(-value))


def project_kernel(
    rows_hbm, gain_hbm, wx_hbm, wz_hbm, out_ref, rows_ref, gain_ref, wx_ref, wz_ref, sems, small_sems
):
    small = [
        pltpu.make_async_copy(rows_hbm, rows_ref, small_sems.at[0]),
        pltpu.make_async_copy(gain_hbm, gain_ref, small_sems.at[1]),
    ]
    for copy in small:
        copy.start()
    copies = []
    for half, (source, target) in enumerate(((wx_hbm, wx_ref), (wz_hbm, wz_ref))):
        copies.append(pltpu.make_async_copy(source, target, sems.at[half]))
        copies[-1].start()
    for copy in small:
        copy.wait()
    rows = rows_ref[...].astype(f32)
    scaled = (rows * gain_ref[...]).astype(bf16)
    column = jnp.sum(rows * rows, axis=1, keepdims=True)
    eye = row_index(ALL_ROWS) == lane_index(ALL_ROWS)
    squares = jnp.sum(jnp.where(eye, column, 0.0), axis=0, keepdims=True)
    hi = rounded(squares)
    which = row_index(8)
    stats = jnp.where(which == 0, hi, jnp.where(which == 1, squares - hi, 0.0))
    for half, weight_ref in enumerate((wx_ref, wz_ref)):
        copies[half].wait()
        part = jnp.dot(scaled, weight_ref[...], preferred_element_type=f32)
        for k in range(out_ref.shape[1]):
            chunk = part[:, k * LANES : (k + 1) * LANES]
            out_ref[half, k] = jnp.concatenate([chunk, stats], axis=0).astype(bf16)


def reduce_kernel(width_all, in_ref, out_ref):
    total = in_ref[0].astype(f32)
    for source in range(1, in_ref.shape[0]):
        total = total + in_ref[source].astype(f32)
    squares = total[ALL_ROWS : ALL_ROWS + 1] + total[ALL_ROWS + 1 : ALL_ROWS + 2]
    eye = row_index(ALL_ROWS) == lane_index(ALL_ROWS)
    column = jnp.sum(jnp.where(eye, squares, 0.0), axis=1, keepdims=True)
    mine = (total[:ALL_ROWS] * lax.rsqrt(column / width_all + 1e-06)).astype(bf16)
    for target in range(out_ref.shape[0]):
        out_ref[target] = mine


def conv_kernel(inner_ref, hist_ref, taps_ref, bias_ref, xp_ref, low_ref, mixed_ref, hist_out_ref, mixed16):
    for k in range(mixed_ref.shape[1] // LANES):
        cols = slice(k * LANES, (k + 1) * LANES)
        fresh = inner_ref[k].astype(f32)
        window = [hist_ref[t, :, cols] for t in range(STEPS)]
        window += [fresh[s * ROWS : (s + 1) * ROWS] for s in range(STEPS)]
        taps = taps_ref[:, cols]
        bias = bias_ref[:, cols]
        mixed = []
        for s in range(STEPS):
            total = window[s] * taps[0:1]
            for t in range(1, STEPS + 1):
                total = total + window[s + t] * taps[t : t + 1]
            mixed.append(silu(total + bias))
            hist_out_ref[s, :, cols] = window[STEPS + s]
        mixed = jnp.concatenate(mixed, axis=0)
        mixed_ref[:, cols] = mixed
        mixed16[:, cols] = mixed.astype(bf16)
    low = lax.dot_general(
        mixed16[...], xp_ref[...], (((1,), (1,)), ((), ())), preferred_element_type=f32
    ).astype(bf16)
    low_ref[...] = low


def scan_kernel(
    own_ref, one_ref, two_ref, three_ref, dt_gain_ref, b_gain_ref, c_gain_ref, dt_bias_ref, a_ref, skip_ref, mixed_ref, gate_ref,
    state_ref, dtp_ref, op_ref, state_out_ref, part_ref, b_wide, c_wide, decay_wide,
):
    tiles = state_ref.shape[0]
    low = sum_refs((own_ref, one_ref, two_ref, three_ref))
    raw = low[:, :DTR]
    mean_sq = jnp.sum(raw * raw, axis=1, keepdims=True) / DTR
    dt_low = (raw * lax.rsqrt(mean_sq + 1e-06) * dt_gain_ref[...]).astype(bf16)
    for wide, gain_ref, at in ((b_wide, b_gain_ref, DTR), (c_wide, c_gain_ref, DTR + DS)):
        raw = low[:, at : at + DS]
        mean_sq = jnp.sum(raw * raw, axis=1, keepdims=True) / DS
        normed = raw * lax.rsqrt(mean_sq + 1e-06) * gain_ref[...]
        for n in range(DS):
            wide[n] = jnp.broadcast_to(normed[:, n : n + 1], (ALL_ROWS, LANES))
    for tile in range(tiles):
        decay = -jnp.exp(a_ref[:, tile * LANES : (tile + 1) * LANES])
        for n in range(DS):
            decay_wide[tile, n] = jnp.broadcast_to(decay[n : n + 1], (ROWS, LANES))
    raw = jnp.dot(dt_low, dtp_ref[...], preferred_element_type=f32) + dt_bias_ref[...]
    steps = jnp.maximum(raw, 0.0) + jnp.log1p(jnp.exp(-jnp.abs(raw)))
    mixed = mixed_ref[...]
    drive = steps * mixed
    scanned = []
    for tile in range(tiles):
        cols = slice(tile * LANES, (tile + 1) * LANES)
        y = [jnp.zeros((ROWS, LANES), f32) for _ in range(STEPS)]
        for n in range(DS):
            state = state_ref[tile, n]
            decay = decay_wide[tile, n]
            for s in range(STEPS):
                rows = slice(s * ROWS, (s + 1) * ROWS)
                state = (
                    jnp.exp(steps[rows, cols] * decay) * state + drive[rows, cols] * b_wide[n, rows]
                )
                y[s] = y[s] + c_wide[n, rows] * state
            state_out_ref[tile, n] = state
        y = jnp.concatenate(y, axis=0) + skip_ref[:, cols] * mixed[:, cols]
        scanned.append((y * silu(gate_ref[tiles + tile].astype(f32))).astype(bf16))
    total = jnp.dot(jnp.concatenate(scanned, axis=1), op_ref[...], preferred_element_type=f32)
    part_ref[...] = total.astype(bf16)


def qkv_kernel(
    own_ref, one_ref, two_ref, three_ref, rows_ref, gain_ref, wq_ref, wk_ref, wv_ref,
    residual_ref, out_ref,
):
    residual = rows_ref[...].astype(f32) + sum_refs((own_ref, one_ref, two_ref, three_ref))
    residual_ref[...] = residual
    scaled = (residual * gain_ref[...]).astype(bf16)
    column = jnp.sum(residual * residual, axis=1, keepdims=True)
    eye = row_index(ALL_ROWS) == lane_index(ALL_ROWS)
    squares = jnp.sum(jnp.where(eye, column, 0.0), axis=0, keepdims=True)
    blocks = []
    for weight_ref in (wq_ref, wk_ref, wv_ref):
        part = jnp.dot(scaled, weight_ref[...], preferred_element_type=f32)
        blocks += [part[:, at : at + HEAD] for at in range(0, part.shape[1], HEAD)]
    out_ref[...] = jnp.concatenate(blocks + [pair_rows(squares)], axis=0).astype(bf16)


def pair_rows(squares):
    hi = rounded(squares)
    which = row_index(8)
    return jnp.where(which == 0, hi, jnp.where(which == 1, squares - hi, 0.0))


def pair_total(total):
    return total[-8:-7] + total[-7:-6]


def sum_refs(refs):
    parts = [ref[...].astype(f32) for ref in refs]
    if len(parts) == 2:
        return parts[0] + parts[1]
    return (parts[0] + parts[1]) + (parts[2] + parts[3])


def qkv_sum_kernel(*refs):
    out_ref = refs[-1]
    total = sum_refs(refs[:-1])
    stats = pair_rows(pair_total(total))
    out_ref[...] = jnp.concatenate([total[:-8], stats], axis=0).astype(bf16)


def pack_logs(logs):
    which = lane_index(ALL_ROWS)
    logs = jnp.where(which < ROWS, logs, 0.0)
    hi = rounded(logs)
    mid = rounded(logs - hi)
    low = logs - hi - mid
    return hi + pltpu.roll(mid, ROWS, 1) + pltpu.roll(low, 2 * ROWS, 1)


def unpack_logs(packed):
    return (
        packed + pltpu.roll(packed, LANES - ROWS, 1) + pltpu.roll(packed, LANES - 2 * ROWS, 1)
    )


def attention_kernel(
    width_all, first_ref, lengths_ref, blocks_ref, own_ref, one_ref, two_ref, three_ref,
    keys_ref, values_ref,
    new_keys_ref, new_values_ref, out_ref, query, fresh_k, fresh_v,
):
    total = sum_refs((own_ref, one_ref, two_ref, three_ref))
    eye = row_index(ALL_ROWS) == lane_index(ALL_ROWS)
    column = jnp.sum(jnp.where(eye, pair_total(total), 0.0), axis=1, keepdims=True)
    scale = lax.rsqrt(column / width_all + 1e-06)
    blocks = [
        rounded(total[at : at + ALL_ROWS] * scale)
        for at in range(0, total.shape[0] - 8, ALL_ROWS)
    ]
    heads = len(blocks) - 2
    queries = STEPS * heads
    keys_now, values_now = blocks[heads:]
    new_keys_ref[...] = keys_now.astype(bf16)
    new_values_ref[...] = values_now.astype(bf16)
    fresh_k[...] = jnp.zeros_like(fresh_k)
    fresh_v[...] = jnp.zeros_like(fresh_v)
    for s in range(STEPS):
        rows = slice(s * ROWS, (s + 1) * ROWS)
        fresh_k[pl.ds(s, ROWS, stride=8), :] = keys_now[rows]
        fresh_v[pl.ds(s, ROWS, stride=8), :] = values_now[rows]
        for g in range(heads):
            query[pl.ds(s * heads + g, ROWS, stride=queries), :] = blocks[g][rows]
    which = lane_index(queries, 8)
    fresh_live = (which * heads <= row_index(queries, 8)) & (which < STEPS)
    fresh_live = fresh_live & (first_ref[0] == 1)
    score_scale = HEAD**-0.5
    lanes = lane_index(queries)
    contract = (((1,), (1,)), ((), ()))
    every = range(ROWS)
    scores, fresh, live = [], [], []
    for b in every:
        query_b = query[b * queries : (b + 1) * queries, :].astype(bf16)
        scores.append(
            lax.dot_general(query_b, keys_ref[b], contract, preferred_element_type=f32)
        )
        fresh.append(
            lax.dot_general(
                query_b,
                fresh_k[b * 8 : (b + 1) * 8, :].astype(bf16),
                contract,
                preferred_element_type=f32,
            )
        )
        live.append(
            jnp.concatenate(
                [
                    lanes < lengths_ref[b] - blocks_ref[k, b] * BLK
                    for k in range(keys_ref.shape[1] // BLK)
                ],
                axis=1,
            )
        )
    scores = [jnp.where(live[b], scores[b] * score_scale, NEGATIVE) for b in every]
    fresh = [jnp.where(fresh_live, fresh[b] * score_scale, NEGATIVE) for b in every]
    peaks = [
        jnp.maximum(
            jnp.max(scores[b], axis=1, keepdims=True), jnp.max(fresh[b], axis=1, keepdims=True)
        )
        for b in every
    ]
    weights = [jnp.where(live[b], jnp.exp(scores[b] - peaks[b]), 0.0) for b in every]
    fresh = [jnp.where(fresh_live, jnp.exp(fresh[b] - peaks[b]), 0.0) for b in every]
    attended = [
        jnp.dot(weights[b].astype(bf16), values_ref[b], preferred_element_type=f32)
        + jnp.dot(
            fresh[b].astype(bf16),
            fresh_v[b * 8 : (b + 1) * 8, :].astype(bf16),
            preferred_element_type=f32,
        )
        for b in every
    ]
    sums = [
        jnp.sum(weights[b], axis=1, keepdims=True) + jnp.sum(fresh[b], axis=1, keepdims=True)
        for b in every
    ]
    logs = jnp.zeros((queries, LANES), f32)
    for b in every:
        any_live = sums[b] > 0
        safe = jnp.where(any_live, sums[b], 1.0)
        out_ref[b] = (attended[b] / safe).astype(bf16)
        log_sum = jnp.where(any_live, peaks[b] + jnp.log(safe), NEGATIVE)
        logs = jnp.where(lanes == b, log_sum, logs)
    out_ref[ROWS] = pack_logs(logs).astype(bf16)


def shares_of(refs):
    logs = [unpack_logs(ref[ROWS].astype(f32)) for ref in refs]
    top = functools.reduce(jnp.maximum, logs)
    shares = [jnp.exp(log - top) for log in logs]
    total = functools.reduce(jnp.add, shares)
    return [share / total for share in shares], top + jnp.log(total)


def combined_row(refs, shares, b):
    attended = [shares[i][:, b : b + 1] * ref[b].astype(f32) for i, ref in enumerate(refs)]
    return functools.reduce(jnp.add, attended)


def combine_kernel(*refs):
    refs, out_ref = refs[:-1], refs[-1]
    shares, logs = shares_of(refs)
    for b in range(ROWS):
        out_ref[b] = combined_row(refs, shares, b).astype(bf16)
    out_ref[ROWS] = pack_logs(logs).astype(bf16)


def finish_kernel(own_ref, one_ref, two_ref, three_ref, weight_ref, out_ref, attended):
    refs = (own_ref, one_ref, two_ref, three_ref)
    shares, _ = shares_of(refs)
    for b in range(ROWS):
        queries = shares[0].shape[0]
        attended[b * queries : (b + 1) * queries, :] = combined_row(refs, shares, b)
    heads = queries // STEPS
    rows = jnp.concatenate(
        [
            jnp.concatenate(
                [
                    attended[pl.ds(s * heads + g, ROWS, stride=queries), :]
                    for g in range(heads)
                ],
                axis=1,
            )
            for s in range(STEPS)
        ],
        axis=0,
    ).astype(bf16)
    part = jnp.dot(rows, weight_ref[...], preferred_element_type=f32).astype(bf16)
    out_ref[...] = part


def body(
    embeds, norm_mamba, in_x, in_z, conv_w, conv_b, x_proj, dt_norm, b_norm, c_norm, dt_proj,
    dt_bias, a_log, d_skip, out_proj, norm_attn, w_query, key_matrix, value_matrix, w_out,
    cache_k, value_cache, lengths, block_of_slot, conv_state, ssm_state,
):
    ctx_size = lax.axis_size(CTX)
    local_width = embeds.shape[2]
    width_all = float(local_width * ctx_size)
    channels = in_x.shape[1]
    heads = w_query.shape[1] // HEAD
    queries = STEPS * heads
    chunk_count = channels // LANES
    rows_in = embeds.reshape(ALL_ROWS, local_width)

    hbm = pl.BlockSpec(memory_space=pltpu.HBM)
    vmem = pl.BlockSpec(memory_space=pltpu.VMEM)
    (chunks,) = call(
        project_kernel,
        [((2, chunk_count, 32, LANES), bf16)],
        rows_in,
        norm_mamba.reshape(1, -1),
        in_x,
        in_z,
        vmem_mib=62,
        in_specs=[hbm] * 4,
        scratch_shapes=[
            pltpu.VMEM((ALL_ROWS, local_width), bf16),
            pltpu.VMEM((1, local_width), f32),
            pltpu.VMEM(in_x.shape, bf16),
            pltpu.VMEM(in_z.shape, bf16),
            pltpu.SemaphoreType.DMA((2,)),
            pltpu.SemaphoreType.DMA((2,)),
        ],
    )
    received = exchange(chunks.reshape(2 * chunk_count, 32, LANES), CTX)
    (mine,) = call(
        functools.partial(reduce_kernel, width_all),
        [((ctx_size, ALL_ROWS, LANES), bf16)],
        received,
    )
    inner = exchange(mine, CTX)

    low, mixed, history = call(
        conv_kernel,
        [
            ((ALL_ROWS, DTR + 2 * DS), bf16),
            ((ALL_ROWS, channels), f32),
            ((STEPS, ROWS, channels), f32),
        ],
        inner,
        conv_state.transpose(1, 0, 2),
        conv_w,
        conv_b.reshape(1, -1),
        x_proj.T,
        scratch_shapes=[pltpu.VMEM((ALL_ROWS, channels), bf16)],
    )
    low = over_cores(low)
    tiled = (chunk_count, DS, ROWS, LANES)
    state = ssm_state.reshape(ROWS, DS, chunk_count, LANES).transpose(2, 1, 0, 3)
    state, part = call(
        scan_kernel,
        [(tiled, f32), ((ALL_ROWS, local_width), bf16)],
        low,
        *from_partners(low, "y"),
        dt_norm.reshape(1, -1),
        b_norm.reshape(1, -1),
        c_norm.reshape(1, -1),
        dt_bias.reshape(1, -1),
        a_log,
        d_skip.reshape(1, -1),
        mixed,
        inner,
        state,
        dt_proj,
        out_proj,
        scratch_shapes=[
            pltpu.VMEM((DS, ALL_ROWS, LANES), f32),
            pltpu.VMEM((DS, ALL_ROWS, LANES), f32),
            pltpu.VMEM(tiled, f32),
        ],
    )
    state = state.transpose(2, 1, 0, 3).reshape(ssm_state.shape)
    part = over_cores(part)

    packed = ((heads + 2) * ALL_ROWS + 8, HEAD)
    residual, projected = call(
        qkv_kernel,
        [((ALL_ROWS, local_width), f32), (packed, bf16)],
        part,
        *from_partners(part, "y"),
        rows_in,
        norm_attn.reshape(1, -1),
        w_query,
        key_matrix,
        value_matrix,
    )
    shape = (packed, bf16)
    (projected,) = call(qkv_sum_kernel, [shape], projected, *from_partners(projected))
    (projected,) = call(qkv_sum_kernel, [shape], projected, from_other(projected, "zb"))
    others = from_partners(projected, "za")
    *others, state = lax.optimization_barrier((*others, state))

    first = (lax.axis_index(CTX) == 0).astype(jnp.int32).reshape(1)
    new_keys, new_values, attended = call(
        functools.partial(attention_kernel, width_all),
        [
            ((ALL_ROWS, HEAD), bf16),
            ((ALL_ROWS, HEAD), bf16),
            ((ROWS + 1, queries, HEAD), bf16),
        ],
        first,
        lengths,
        block_of_slot.T,
        projected,
        *others,
        cache_k,
        value_cache,
        in_specs=[pl.BlockSpec(memory_space=pltpu.SMEM)] * 3 + [vmem] * 6,
        scratch_shapes=[
            pltpu.VMEM((ROWS * queries, HEAD), f32),
            pltpu.VMEM((ROWS * 8, HEAD), f32),
            pltpu.VMEM((ROWS * 8, HEAD), f32),
        ],
    )
    shape = (attended.shape, bf16)
    (attended,) = call(combine_kernel, [shape], attended, *from_partners(attended))
    (attended,) = call(combine_kernel, [shape], attended, from_other(attended, "zb"))
    (part,) = call(
        finish_kernel,
        [((ALL_ROWS, local_width), bf16)],
        attended,
        *from_partners(attended, "za"),
        w_out,
        scratch_shapes=[pltpu.VMEM((ROWS * queries, HEAD), f32)],
    )
    part = over_cores(part)
    one, two, three = (other.astype(f32) for other in from_partners(part, "y"))
    hidden = residual + ((part.astype(f32) + one) + (two + three))
    return (
        hidden.reshape(STEPS, ROWS, local_width),
        new_keys.reshape(STEPS, ROWS, HEAD),
        new_values.reshape(STEPS, ROWS, HEAD),
        state,
        history.transpose(1, 0, 2),
    )


def solution(mesh):
    ctx_size, tp_size = mesh.devices.shape
    split = Mesh(
        mesh.devices.reshape(ctx_size // X_SIZE // 2, 2, X_SIZE, tp_size // 2, 2),
        ("za", "zb", "x", "y", "core"),
    )
    return jax.shard_map(
        body,
        mesh=split,
        in_specs=(
            P(None, None, CTX),
            P(CTX),
            P(CTX, TP),
            P(CTX, TP),
            P(None, TP),
            P(TP),
            P(TP, None),
            P(),
            P(),
            P(),
            P(None, TP),
            P(TP),
            P(None, TP),
            P(TP),
            P(TP, CTX),
            P(CTX),
            P(CTX, TP),
            P(CTX, TP),
            P(CTX, TP),
            P(TP, CTX),
            P(None, CTX, TP),
            P(None, CTX, TP),
            P(),
            P(None, CTX),
            P(None, None, TP),
            P(None, None, TP),
        ),
        out_specs=(
            P(None, None, CTX),
            P(None, None, TP),
            P(None, None, TP),
            P(None, None, TP),
            P(None, None, TP),
        ),
        check_vma=False,
    )
```

```python
import functools

import jax
import jax.numpy as jnp
from jax import lax
from jax.experimental import pallas as pl
from jax.experimental.pallas import tpu as pltpu
from jax.sharding import Mesh, PartitionSpec as P

DS = 16
DTR = 512
HEAD = 128
BLK = 128
STEPS = 3
ROWS = 8
ALL_ROWS = STEPS * ROWS
LANES = 128
X_SIZE = 4
CTX = ("za", "zb", "x")
TP = ("y", "core")
FLOPS = 3_000_000_000
NEGATIVE = -1e30
bf16 = jnp.bfloat16
f32 = jnp.float32


def exchange(parts, axis):
    return lax.all_to_all(parts, axis, 0, 0, tiled=True)


def from_partners(part, axis="x"):
    received = {
        flip: lax.ppermute(part, axis, [(i, i ^ flip) for i in range(4)]) for flip in (1, 3, 2)
    }
    return received[1], received[2], received[3]


def from_other(part, axis):
    return lax.ppermute(part, axis, [(0, 1), (1, 0)])


def over_cores(part):
    return part + from_other(part, "core")


def call(kernel, outs, *operands, vmem_mib=48, **options):
    return pl.pallas_call(
        kernel,
        out_shape=[jax.ShapeDtypeStruct(shape, dtype) for shape, dtype in outs],
        compiler_params=pltpu.CompilerParams(vmem_limit_bytes=vmem_mib * 1024 * 1024),
        cost_estimate=pl.CostEstimate(flops=FLOPS, bytes_accessed=8 << 20, transcendentals=0),
        **options,
    )(*operands)


def lane_index(rows, lanes=LANES):
    return lax.broadcasted_iota(jnp.int32, (rows, lanes), 1)


def row_index(rows, lanes=LANES):
    return lax.broadcasted_iota(jnp.int32, (rows, lanes), 0)


def rounded(value):
    return value.astype(bf16).astype(f32)


def silu(value):
    return value / (1.0 + jnp.exp(-value))


def project_kernel(
    rows_hbm, gain_hbm, wx_hbm, wz_hbm, out_ref, rows_ref, gain_ref, wx_ref, wz_ref, sems, small_sems
):
    small = [
        pltpu.make_async_copy(rows_hbm, rows_ref, small_sems.at[0]),
        pltpu.make_async_copy(gain_hbm, gain_ref, small_sems.at[1]),
    ]
    for copy in small:
        copy.start()
    copies = []
    for half, (source, target) in enumerate(((wx_hbm, wx_ref), (wz_hbm, wz_ref))):
        copies.append(pltpu.make_async_copy(source, target, sems.at[half]))
        copies[-1].start()
    for copy in small:
        copy.wait()
    rows = rows_ref[...].astype(f32)
    scaled = (rows * gain_ref[...]).astype(bf16)
    column = jnp.sum(rows * rows, axis=1, keepdims=True)
    eye = row_index(ALL_ROWS) == lane_index(ALL_ROWS)
    squares = jnp.sum(jnp.where(eye, column, 0.0), axis=0, keepdims=True)
    hi = rounded(squares)
    which = row_index(8)
    stats = jnp.where(which == 0, hi, jnp.where(which == 1, squares - hi, 0.0))
    for half, weight_ref in enumerate((wx_ref, wz_ref)):
        copies[half].wait()
        part = jnp.dot(scaled, weight_ref[...], preferred_element_type=f32)
        for k in range(out_ref.shape[1]):
            chunk = part[:, k * LANES : (k + 1) * LANES]
            out_ref[half, k] = jnp.concatenate([chunk, stats], axis=0).astype(bf16)


def reduce_kernel(width_all, in_ref, out_ref):
    total = in_ref[0].astype(f32)
    for source in range(1, in_ref.shape[0]):
        total = total + in_ref[source].astype(f32)
    squares = total[ALL_ROWS : ALL_ROWS + 1] + total[ALL_ROWS + 1 : ALL_ROWS + 2]
    eye = row_index(ALL_ROWS) == lane_index(ALL_ROWS)
    column = jnp.sum(jnp.where(eye, squares, 0.0), axis=1, keepdims=True)
    mine = (total[:ALL_ROWS] * lax.rsqrt(column / width_all + 1e-06)).astype(bf16)
    for target in range(out_ref.shape[0]):
        out_ref[target] = mine


def conv_kernel(inner_ref, hist_ref, taps_ref, bias_ref, xp_ref, low_ref, mixed_ref, hist_out_ref, mixed16):
    for k in range(mixed_ref.shape[1] // LANES):
        cols = slice(k * LANES, (k + 1) * LANES)
        fresh = inner_ref[k].astype(f32)
        window = [hist_ref[t, :, cols] for t in range(STEPS)]
        window += [fresh[s * ROWS : (s + 1) * ROWS] for s in range(STEPS)]
        taps = taps_ref[:, cols]
        bias = bias_ref[:, cols]
        mixed = []
        for s in range(STEPS):
            total = window[s] * taps[0:1]
            for t in range(1, STEPS + 1):
                total = total + window[s + t] * taps[t : t + 1]
            mixed.append(silu(total + bias))
            hist_out_ref[s, :, cols] = window[STEPS + s]
        mixed = jnp.concatenate(mixed, axis=0)
        mixed_ref[:, cols] = mixed
        mixed16[:, cols] = mixed.astype(bf16)
    low = lax.dot_general(
        mixed16[...], xp_ref[...], (((1,), (1,)), ((), ())), preferred_element_type=f32
    ).astype(bf16)
    low_ref[...] = low


def scan_kernel(
    own_ref, one_ref, two_ref, three_ref, dt_gain_ref, b_gain_ref, c_gain_ref, dt_bias_ref, a_ref, skip_ref, mixed_ref, gate_ref,
    state_ref, dtp_ref, op_ref, state_out_ref, part_ref, b_wide, c_wide, decay_wide,
):
    tiles = state_ref.shape[0]
    low = sum_refs((own_ref, one_ref, two_ref, three_ref))
    raw = low[:, :DTR]
    mean_sq = jnp.sum(raw * raw, axis=1, keepdims=True) / DTR
    dt_low = (raw * lax.rsqrt(mean_sq + 1e-06) * dt_gain_ref[...]).astype(bf16)
    for wide, gain_ref, at in ((b_wide, b_gain_ref, DTR), (c_wide, c_gain_ref, DTR + DS)):
        raw = low[:, at : at + DS]
        mean_sq = jnp.sum(raw * raw, axis=1, keepdims=True) / DS
        normed = raw * lax.rsqrt(mean_sq + 1e-06) * gain_ref[...]
        for n in range(DS):
            wide[n] = jnp.broadcast_to(normed[:, n : n + 1], (ALL_ROWS, LANES))
    for tile in range(tiles):
        decay = -jnp.exp(a_ref[:, tile * LANES : (tile + 1) * LANES])
        for n in range(DS):
            decay_wide[tile, n] = jnp.broadcast_to(decay[n : n + 1], (ROWS, LANES))
    raw = jnp.dot(dt_low, dtp_ref[...], preferred_element_type=f32) + dt_bias_ref[...]
    steps = jnp.maximum(raw, 0.0) + jnp.log1p(jnp.exp(-jnp.abs(raw)))
    mixed = mixed_ref[...]
    drive = steps * mixed
    scanned = []
    for tile in range(tiles):
        cols = slice(tile * LANES, (tile + 1) * LANES)
        y = [jnp.zeros((ROWS, LANES), f32) for _ in range(STEPS)]
        for n in range(DS):
            state = state_ref[tile, n]
            decay = decay_wide[tile, n]
            for s in range(STEPS):
                rows = slice(s * ROWS, (s + 1) * ROWS)
                state = (
                    jnp.exp(steps[rows, cols] * decay) * state + drive[rows, cols] * b_wide[n, rows]
                )
                y[s] = y[s] + c_wide[n, rows] * state
            state_out_ref[tile, n] = state
        y = jnp.concatenate(y, axis=0) + skip_ref[:, cols] * mixed[:, cols]
        scanned.append((y * silu(gate_ref[tiles + tile].astype(f32))).astype(bf16))
    total = jnp.dot(jnp.concatenate(scanned, axis=1), op_ref[...], preferred_element_type=f32)
    part_ref[...] = total.astype(bf16)


def qkv_kernel(
    own_ref, one_ref, two_ref, three_ref, rows_ref, gain_ref, wq_ref, wk_ref, wv_ref,
    residual_ref, out_ref,
):
    residual = rows_ref[...].astype(f32) + sum_refs((own_ref, one_ref, two_ref, three_ref))
    residual_ref[...] = residual
    scaled = (residual * gain_ref[...]).astype(bf16)
    column = jnp.sum(residual * residual, axis=1, keepdims=True)
    eye = row_index(ALL_ROWS) == lane_index(ALL_ROWS)
    squares = jnp.sum(jnp.where(eye, column, 0.0), axis=0, keepdims=True)
    blocks = []
    for weight_ref in (wq_ref, wk_ref, wv_ref):
        part = jnp.dot(scaled, weight_ref[...], preferred_element_type=f32)
        blocks += [part[:, at : at + HEAD] for at in range(0, part.shape[1], HEAD)]
    out_ref[...] = jnp.concatenate(blocks + [pair_rows(squares)], axis=0).astype(bf16)


def pair_rows(squares):
    hi = rounded(squares)
    which = row_index(8)
    return jnp.where(which == 0, hi, jnp.where(which == 1, squares - hi, 0.0))


def pair_total(total):
    return total[-8:-7] + total[-7:-6]


def sum_refs(refs):
    parts = [ref[...].astype(f32) for ref in refs]
    if len(parts) == 2:
        return parts[0] + parts[1]
    return (parts[0] + parts[1]) + (parts[2] + parts[3])


def qkv_sum_kernel(*refs):
    out_ref = refs[-1]
    total = sum_refs(refs[:-1])
    stats = pair_rows(pair_total(total))
    out_ref[...] = jnp.concatenate([total[:-8], stats], axis=0).astype(bf16)


def pack_logs(logs):
    logs = jnp.where(lane_index(ROWS) < 32, logs, 0.0)
    hi = rounded(logs)
    mid = rounded(logs - hi)
    low = logs - hi - mid
    return hi + pltpu.roll(mid, 32, 1) + pltpu.roll(low, 64, 1)


def unpack_logs(packed):
    return packed + pltpu.roll(packed, LANES - 32, 1) + pltpu.roll(packed, LANES - 64, 1)


def attention_kernel(
    width_all, first_ref, lengths_ref, blocks_ref, own_ref, one_ref, two_ref, three_ref,
    keys_ref, values_ref,
    new_keys_ref, new_values_ref, out_ref, query, fresh_k, fresh_v,
):
    total = sum_refs((own_ref, one_ref, two_ref, three_ref))
    eye = row_index(ALL_ROWS) == lane_index(ALL_ROWS)
    column = jnp.sum(jnp.where(eye, pair_total(total), 0.0), axis=1, keepdims=True)
    scale = lax.rsqrt(column / width_all + 1e-06)
    blocks = [
        rounded(total[at : at + ALL_ROWS] * scale)
        for at in range(0, total.shape[0] - 8, ALL_ROWS)
    ]
    heads = len(blocks) - 2
    queries = STEPS * heads
    keys_now, values_now = blocks[heads:]
    new_keys_ref[...] = keys_now.astype(bf16)
    new_values_ref[...] = values_now.astype(bf16)
    fresh_k[...] = jnp.zeros_like(fresh_k)
    fresh_v[...] = jnp.zeros_like(fresh_v)
    for s in range(STEPS):
        rows = slice(s * ROWS, (s + 1) * ROWS)
        fresh_k[pl.ds(s, ROWS, stride=8), :] = keys_now[rows]
        fresh_v[pl.ds(s, ROWS, stride=8), :] = values_now[rows]
        for g in range(heads):
            query[pl.ds(s * heads + g, ROWS, stride=queries), :] = blocks[g][rows]
    which = lane_index(queries, 8)
    fresh_live = (which * heads <= row_index(queries, 8)) & (which < STEPS)
    fresh_live = fresh_live & (first_ref[0] == 1)
    score_scale = HEAD**-0.5
    lanes = lane_index(queries)
    contract = (((1,), (1,)), ((), ()))
    every = range(ROWS)
    scores, fresh, live = [], [], []
    for b in every:
        query_b = query[b * queries : (b + 1) * queries, :].astype(bf16)
        scores.append(
            lax.dot_general(query_b, keys_ref[b], contract, preferred_element_type=f32)
        )
        fresh.append(
            lax.dot_general(
                query_b,
                fresh_k[b * 8 : (b + 1) * 8, :].astype(bf16),
                contract,
                preferred_element_type=f32,
            )
        )
        live.append(
            jnp.concatenate(
                [
                    lanes < lengths_ref[b] - blocks_ref[k, b] * BLK
                    for k in range(keys_ref.shape[1] // BLK)
                ],
                axis=1,
            )
        )
    scores = [jnp.where(live[b], scores[b] * score_scale, NEGATIVE) for b in every]
    fresh = [jnp.where(fresh_live, fresh[b] * score_scale, NEGATIVE) for b in every]
    peaks = [
        jnp.maximum(
            jnp.max(scores[b], axis=1, keepdims=True), jnp.max(fresh[b], axis=1, keepdims=True)
        )
        for b in every
    ]
    weights = [jnp.where(live[b], jnp.exp(scores[b] - peaks[b]), 0.0) for b in every]
    fresh = [jnp.where(fresh_live, jnp.exp(fresh[b] - peaks[b]), 0.0) for b in every]
    attended = [
        jnp.dot(weights[b].astype(bf16), values_ref[b], preferred_element_type=f32)
        + jnp.dot(
            fresh[b].astype(bf16),
            fresh_v[b * 8 : (b + 1) * 8, :].astype(bf16),
            preferred_element_type=f32,
        )
        for b in every
    ]
    sums = [
        jnp.sum(weights[b], axis=1, keepdims=True) + jnp.sum(fresh[b], axis=1, keepdims=True)
        for b in every
    ]
    eye = lanes == row_index(queries)
    blocks, logs = [], []
    for b in every:
        any_live = sums[b] > 0
        safe = jnp.where(any_live, sums[b], 1.0)
        blocks.append(attended[b] / safe)
        log_sum = jnp.where(any_live, peaks[b] + jnp.log(safe), NEGATIVE)
        logs.append(jnp.sum(jnp.where(eye, log_sum, 0.0), axis=0, keepdims=True))
    blocks.append(pack_logs(jnp.concatenate(logs, axis=0)))
    out_ref[...] = jnp.concatenate(blocks, axis=0).astype(bf16)


def combined(refs):
    parts = [ref[...].astype(f32) for ref in refs]
    logs = [unpack_logs(part[-ROWS:]) for part in parts]
    top = functools.reduce(jnp.maximum, logs)
    shares = [jnp.exp(log - top) for log in logs]
    total = functools.reduce(jnp.add, shares)
    shares = [share / total for share in shares]
    queries = (parts[0].shape[0] - ROWS) // ROWS
    eye = lane_index(queries) == row_index(queries)
    blocks = []
    for b in range(ROWS):
        block = None
        for part, share in zip(parts, shares):
            column = jnp.sum(jnp.where(eye, share[b : b + 1], 0.0), axis=1, keepdims=True)
            term = column * part[b * queries : (b + 1) * queries]
            block = term if block is None else block + term
        blocks.append(block)
    return blocks, top + jnp.log(total)


def combine_kernel(*refs):
    blocks, logs = combined(refs[:-1])
    refs[-1][...] = jnp.concatenate(blocks + [pack_logs(logs)], axis=0).astype(bf16)


def finish_kernel(own_ref, one_ref, two_ref, three_ref, weight_ref, out_ref, attended):
    blocks, _ = combined((own_ref, one_ref, two_ref, three_ref))
    queries = blocks[0].shape[0]
    attended[...] = jnp.concatenate(blocks, axis=0)
    heads = queries // STEPS
    rows = jnp.concatenate(
        [
            jnp.concatenate(
                [
                    attended[pl.ds(s * heads + g, ROWS, stride=queries), :]
                    for g in range(heads)
                ],
                axis=1,
            )
            for s in range(STEPS)
        ],
        axis=0,
    ).astype(bf16)
    part = jnp.dot(rows, weight_ref[...], preferred_element_type=f32).astype(bf16)
    out_ref[...] = part


def body(
    embeds, norm_mamba, in_x, in_z, conv_w, conv_b, x_proj, dt_norm, b_norm, c_norm, dt_proj,
    dt_bias, a_log, d_skip, out_proj, norm_attn, w_query, key_matrix, value_matrix, w_out,
    cache_k, value_cache, lengths, block_of_slot, conv_state, ssm_state,
):
    ctx_size = lax.axis_size(CTX)
    local_width = embeds.shape[2]
    width_all = float(local_width * ctx_size)
    channels = in_x.shape[1]
    heads = w_query.shape[1] // HEAD
    queries = STEPS * heads
    chunk_count = channels // LANES
    rows_in = embeds.reshape(ALL_ROWS, local_width)

    hbm = pl.BlockSpec(memory_space=pltpu.HBM)
    vmem = pl.BlockSpec(memory_space=pltpu.VMEM)
    (chunks,) = call(
        project_kernel,
        [((2, chunk_count, 32, LANES), bf16)],
        rows_in,
        norm_mamba.reshape(1, -1),
        in_x,
        in_z,
        vmem_mib=62,
        in_specs=[hbm] * 4,
        scratch_shapes=[
            pltpu.VMEM((ALL_ROWS, local_width), bf16),
            pltpu.VMEM((1, local_width), f32),
            pltpu.VMEM(in_x.shape, bf16),
            pltpu.VMEM(in_z.shape, bf16),
            pltpu.SemaphoreType.DMA((2,)),
            pltpu.SemaphoreType.DMA((2,)),
        ],
    )
    received = exchange(chunks.reshape(2 * chunk_count, 32, LANES), CTX)
    (mine,) = call(
        functools.partial(reduce_kernel, width_all),
        [((ctx_size, ALL_ROWS, LANES), bf16)],
        received,
    )
    inner = exchange(mine, CTX)

    low, mixed, history = call(
        conv_kernel,
        [
            ((ALL_ROWS, DTR + 2 * DS), bf16),
            ((ALL_ROWS, channels), f32),
            ((STEPS, ROWS, channels), f32),
        ],
        inner,
        conv_state.transpose(1, 0, 2),
        conv_w,
        conv_b.reshape(1, -1),
        x_proj.T,
        scratch_shapes=[pltpu.VMEM((ALL_ROWS, channels), bf16)],
    )
    low = over_cores(low)
    tiled = (chunk_count, DS, ROWS, LANES)
    state = ssm_state.reshape(ROWS, DS, chunk_count, LANES).transpose(2, 1, 0, 3)
    state, part = call(
        scan_kernel,
        [(tiled, f32), ((ALL_ROWS, local_width), bf16)],
        low,
        *from_partners(low, "y"),
        dt_norm.reshape(1, -1),
        b_norm.reshape(1, -1),
        c_norm.reshape(1, -1),
        dt_bias.reshape(1, -1),
        a_log,
        d_skip.reshape(1, -1),
        mixed,
        inner,
        state,
        dt_proj,
        out_proj,
        scratch_shapes=[
            pltpu.VMEM((DS, ALL_ROWS, LANES), f32),
            pltpu.VMEM((DS, ALL_ROWS, LANES), f32),
            pltpu.VMEM(tiled, f32),
        ],
    )
    state = state.transpose(2, 1, 0, 3).reshape(ssm_state.shape)
    part = over_cores(part)

    packed = ((heads + 2) * ALL_ROWS + 8, HEAD)
    residual, projected = call(
        qkv_kernel,
        [((ALL_ROWS, local_width), f32), (packed, bf16)],
        part,
        *from_partners(part, "y"),
        rows_in,
        norm_attn.reshape(1, -1),
        w_query,
        key_matrix,
        value_matrix,
    )
    shape = (packed, bf16)
    (projected,) = call(qkv_sum_kernel, [shape], projected, *from_partners(projected))
    (projected,) = call(qkv_sum_kernel, [shape], projected, from_other(projected, "zb"))
    others = from_partners(projected, "za")
    *others, state = lax.optimization_barrier((*others, state))

    first = (lax.axis_index(CTX) == 0).astype(jnp.int32).reshape(1)
    new_keys, new_values, attended = call(
        functools.partial(attention_kernel, width_all),
        [
            ((ALL_ROWS, HEAD), bf16),
            ((ALL_ROWS, HEAD), bf16),
            ((ROWS * queries + ROWS, HEAD), bf16),
        ],
        first,
        lengths,
        block_of_slot.T,
        projected,
        *others,
        cache_k,
        value_cache,
        in_specs=[pl.BlockSpec(memory_space=pltpu.SMEM)] * 3 + [vmem] * 6,
        scratch_shapes=[
            pltpu.VMEM((ROWS * queries, HEAD), f32),
            pltpu.VMEM((ROWS * 8, HEAD), f32),
            pltpu.VMEM((ROWS * 8, HEAD), f32),
        ],
    )
    shape = (attended.shape, bf16)
    (attended,) = call(combine_kernel, [shape], attended, *from_partners(attended))
    (attended,) = call(combine_kernel, [shape], attended, from_other(attended, "zb"))
    (part,) = call(
        finish_kernel,
        [((ALL_ROWS, local_width), bf16)],
        attended,
        *from_partners(attended, "za"),
        w_out,
        scratch_shapes=[pltpu.VMEM((ROWS * queries, HEAD), f32)],
    )
    part = over_cores(part)
    one, two, three = (other.astype(f32) for other in from_partners(part, "y"))
    hidden = residual + ((part.astype(f32) + one) + (two + three))
    return (
        hidden.reshape(STEPS, ROWS, local_width),
        new_keys.reshape(STEPS, ROWS, HEAD),
        new_values.reshape(STEPS, ROWS, HEAD),
        state,
        history.transpose(1, 0, 2),
    )


def solution(mesh):
    ctx_size, tp_size = mesh.devices.shape
    split = Mesh(
        mesh.devices.reshape(ctx_size // X_SIZE // 2, 2, X_SIZE, tp_size // 2, 2),
        ("za", "zb", "x", "y", "core"),
    )
    return jax.shard_map(
        body,
        mesh=split,
        in_specs=(
            P(None, None, CTX),
            P(CTX),
            P(CTX, TP),
            P(CTX, TP),
            P(None, TP),
            P(TP),
            P(TP, None),
            P(),
            P(),
            P(),
            P(None, TP),
            P(TP),
            P(None, TP),
            P(TP),
            P(TP, CTX),
            P(CTX),
            P(CTX, TP),
            P(CTX, TP),
            P(CTX, TP),
            P(TP, CTX),
            P(None, CTX, TP),
            P(None, CTX, TP),
            P(),
            P(None, CTX),
            P(None, None, TP),
            P(None, None, TP),
        ),
        out_specs=(
            P(None, None, CTX),
            P(None, None, TP),
            P(None, None, TP),
            P(None, None, TP),
            P(None, None, TP),
        ),
        check_vma=False,
    )
```
